32 devices in a mesh: depth: 8 (over z, x), dp: 4 (over y, core).
Axes of the slice: x: 2, y: 2, z: 4, core: 2. Of those that a mesh axis runs over, the one named last changes fastest.
Arguments:
- cpoints: float32 [8, 4, 64, 256], P('depth', 'dp'), may hold values from -6 to 6, as said below
- weights: bfloat16 [32, 64, 576], P('depth'), may hold values from -0.75 to 0.75
- coarse_gain: float32 [8, 64], P('depth'), may hold values from 0.04 to 1
- cotangent: float32 [8, 4, 64, 256], P('depth', 'dp'), may hold values from -0.6 to 0.6
Outputs:
- corrected: float32 [8, 4, 64, 256], P('depth', 'dp')
- grad_cpoints: float32 [8, 4, 64, 256], P('depth', 'dp')
- grad_weights: float32 [32, 64, 576], P('depth')
The draws below stay inside these ranges and needn't reach their ends.
Inputs may be any that keep to these rules, and one draw needn't show every extreme that they name: cpoints[0] holds the network input; cpoints[d] the current guess of the state entering block d.
All inputs are finite; a program needn't handle non-finite values.
Results may differ from the reference program's by a relative error of at most 0.0041.
Values sent between devices are 32-bit elements; how exact they have to be, the bound alone decides.
A program may use at most 64 MiB of HBM per device.

```python
import math
import jax
import jax.numpy as jnp
from jax import lax

CHANNEL_COUNT = 64
LAYERS_DEV = 4
WID = 16
PIXELS = 256
LAYER_BLOCKS = 8
LAYERS = 32
IMAGES = 4


def draw_cpoints(key, part):
    shape_all = (LAYER_BLOCKS, IMAGES, CHANNEL_COUNT, PIXELS)
    first_key = jax.random.fold_in(key, 0)
    leading = jnp.arange(LAYER_BLOCKS)[:, None, None, None] == 0
    base = jnp.clip(jax.random.normal(first_key, shape_all, jnp.float32), -6.0, 6.0)
    return jnp.where(leading, base, 0.5 * base)


def draw_coarse_gain(key, part):
    random_split_keys = jax.random.split(key, 6)
    slow_share = 0.5
    chooser = jax.random.uniform(random_split_keys[0], (1, CHANNEL_COUNT), jnp.float32)
    slow_scale = jax.random.uniform(random_split_keys[1], (1, CHANNEL_COUNT), jnp.float32, 0.1, 0.4)
    fast_scale = jax.random.uniform(random_split_keys[2], (1, CHANNEL_COUNT), jnp.float32, 0.3, 1.5)
    factor = jnp.exp(jax.random.uniform(random_split_keys[3], (LAYER_BLOCKS, CHANNEL_COUNT), jnp.float32, -0.7, 0.7))
    coarse_rate = jnp.exp(math.log(0.1) * slow_scale * factor / LAYER_BLOCKS)
    fast_rate = jnp.exp(-fast_scale * factor)
    relaxation_sweep = jax.random.uniform(random_split_keys[4], (LAYER_BLOCKS, 1), jnp.float32) < 3.0 / LAYER_BLOCKS
    sweep_boundary = jax.random.uniform(random_split_keys[5], (LAYER_BLOCKS, CHANNEL_COUNT), jnp.float32, 0.5, 0.8)
    coarse_rate = jnp.where(relaxation_sweep, coarse_rate * sweep_boundary, coarse_rate)
    return jnp.where(chooser < slow_share, coarse_rate, fast_rate)


def shard_levels(own_key, shape, cuts, smallest, top_value):
    factor_of, own = 1.0, jax.random.fold_in(own_key, 6)
    for position, shards_of in cuts:
        draws = jnp.exp(jax.random.uniform(jax.random.fold_in(own, position), (shards_of,), jnp.float32, smallest / len(cuts), top_value / len(cuts)))
        factor_of = factor_of * jnp.repeat(draws, shape[position] // shards_of).reshape([-1 if axis == position else 1 for axis in range(len(shape))])
    return factor_of


def scatter_about(rng, dims, scale, limit, shards=(), dtype=jnp.bfloat16):
    result = scale * jax.random.normal(rng, dims, jnp.float32)
    if shards:
        result = result * shard_levels(rng, dims, shards, -0.22, 0.18)
    return jnp.clip(result, -limit, limit).astype(dtype)


def setup_inputs(seed: int = 0) -> dict:
    seeds = jax.random.split(jax.random.key(seed), 5)
    return {
        "cpoints": draw_cpoints(jax.random.fold_in(seeds[4], 71), 0),
        "weights": scatter_about(seeds[1], (LAYERS, CHANNEL_COUNT, 9 * CHANNEL_COUNT), (LAYERS * (900 * CHANNEL_COUNT) ** -0.5), 0.75, ((0, 8),)),
        "coarse_gain": draw_coarse_gain(jax.random.fold_in(seeds[4], 71), 0),
        "cotangent": scatter_about(seeds[3], (LAYER_BLOCKS, IMAGES, CHANNEL_COUNT, PIXELS), 0.1, 0.6, ((0, 8), (1, 4)), jnp.float32),
    }


TAP_OFFSETS = [(-1, -1), (-1, 0), (-1, 1), (0, -1), (0, 0), (0, 1), (1, -1), (1, 0), (1, 1)]


def shift_pixels(values, shift_down, shift_right, row_width):
    pixel_count = values.shape[-1]
    offset = shift_down * row_width + shift_right
    padded = jnp.pad(values, [(0, 0)] * (values.ndim - 1) + [(row_width + 1, row_width + 1)])
    shifted = lax.slice_in_dim(padded, row_width + 1 + offset, row_width + 1 + offset + pixel_count, axis=values.ndim - 1)
    column = jnp.arange(pixel_count) % row_width + shift_right
    inside = (column >= 0) & (column < row_width)
    return jnp.where(inside, shifted, jnp.zeros_like(shifted))


def unfold(values, row_width):
    return jnp.concatenate([shift_pixels(values, a, b, row_width) for a, b in TAP_OFFSETS], axis=1)


def fold_taps(tap_grads, row_width):
    channels = tap_grads.shape[1] // 9
    accumulated = jnp.zeros((tap_grads.shape[0], channels, tap_grads.shape[2]), jnp.float32)
    for tap_index, (a, b) in enumerate(TAP_OFFSETS):
        piece = tap_grads[:, tap_index * channels:(tap_index + 1) * channels]
        accumulated = accumulated + shift_pixels(piece, -a, -b, row_width)
    return accumulated


def layer_forward(current, weight, step_size):
    squashed = jnp.tanh(current)
    patches = unfold(squashed.astype(jnp.bfloat16), WID)
    mixed = jnp.einsum("ok,bkp->bop", weight.astype(jnp.float32), patches.astype(jnp.float32))
    return current + step_size * mixed


def forward_block_pass(current, block_weights, step_size):
    for layer in range(LAYERS_DEV):
        current = layer_forward(current, block_weights[layer], step_size)
    return current


def block_backward(current, block_weights, upstream, step_size):
    inputs_kept = []
    for layer in range(LAYERS_DEV):
        inputs_kept.append(current)
        current = layer_forward(current, block_weights[layer], step_size)
    layer_grads = [None] * LAYERS_DEV
    for layer in reversed(range(LAYERS_DEV)):
        squashed = jnp.tanh(inputs_kept[layer])
        patches = unfold(squashed.astype(jnp.bfloat16), WID).astype(jnp.float32)
        scaled = (step_size * upstream).astype(jnp.bfloat16).astype(jnp.float32)
        layer_grads[layer] = jnp.einsum("bop,bkp->ok", scaled, patches)
        spread = jnp.einsum("ok,bop->bkp", block_weights[layer].astype(jnp.float32), scaled)
        upstream = upstream + (1.0 - squashed * squashed) * fold_taps(spread, WID)
    return upstream, jnp.stack(layer_grads)


def reference(cpoints, weights, coarse_gain, cotangent):
    step_size = 1.0 / LAYERS
    blocks = weights.reshape(LAYER_BLOCKS, LAYERS_DEV, CHANNEL_COUNT, 9 * CHANNEL_COUNT)
    relaxed = lax.map(lambda inputs_pair: forward_block_pass(inputs_pair[0], inputs_pair[1], step_size), (cpoints, blocks))
    start_state = jnp.concatenate([cpoints[:1], relaxed[:-1]], axis=0)
    propagated = lax.map(lambda inputs_pair: forward_block_pass(inputs_pair[0], inputs_pair[1], step_size), (start_state, blocks))
    first_block = (jnp.arange(LAYER_BLOCKS) == 0)[:, None, None, None]
    gained_start = coarse_gain[:, None, :, None] * start_state
    offset = propagated - jnp.where(first_block, jnp.zeros_like(gained_start), gained_start)

    def forward_step(carried_in, inputs_pair):
        rate_vec, increment = inputs_pair
        leaving = rate_vec[None, :, None] * carried_in + increment
        return leaving, leaving

    _, corrected = lax.scan(forward_step, jnp.zeros_like(offset[0]), (coarse_gain, offset))

    def adjoint_step(carried_in, inputs_pair):
        rate_vec, incoming = inputs_pair
        adjoint_here = incoming + carried_in
        return rate_vec[None, :, None] * adjoint_here, (adjoint_here, carried_in)

    _, (adjoints, passed_back) = lax.scan(adjoint_step, jnp.zeros_like(cotangent[0]), (coarse_gain, cotangent), reverse=True)
    back_start, start_grads = lax.map(lambda inputs_trio: block_backward(inputs_trio[0], inputs_trio[1], inputs_trio[2], step_size), (start_state, blocks, adjoints))
    successor_block = jnp.concatenate([back_start[1:], jnp.zeros_like(back_start[:1])], axis=0)
    relaxed_bar = successor_block - passed_back
    back_own, own_grads = lax.map(lambda inputs_trio: block_backward(inputs_trio[0], inputs_trio[1], inputs_trio[2], step_size), (cpoints, blocks, relaxed_bar))
    grad_cpoints = back_own.at[0].add(back_start[0])
    grad_weights = (start_grads + own_grads).reshape(LAYERS, CHANNEL_COUNT, 9 * CHANNEL_COUNT)
    return (corrected, grad_cpoints, grad_weights)
```

```python
import functools

import jax
import jax.numpy as jnp
from jax import lax
from jax.experimental import pallas as pl
from jax.experimental.pallas import tpu as pltpu
from jax.sharding import PartitionSpec as P

MESH = pl.DeviceIdType.MESH
WID = 16
TAP_OFFSETS = [(-1, -1), (-1, 0), (-1, 1), (0, -1), (0, 0), (0, 1), (1, -1), (1, 0), (1, 1)]


def kernel(
    depth,
    dp,
    cp_ref,
    w_ref,
    gain_ref,
    cot_ref,
    corr_ref,
    gcp_ref,
    gw_ref,
    patches,
    slopes,
    back_patches,
    turned,
    start_grads,
    relaxed_buf,
    start_buf,
    back_buf,
    bar_buf,
    passed_buf,
    gains,
    gains_in,
    adj_out,
    adj_in,
    fwd,
    fwd_in,
    sum_a,
    sum_b,
    part_a,
    part_b,
    gain_send,
    gain_recv,
    adj_send,
    adj_recv,
    fwd_send,
    fwd_recv,
    edge_send,
    edge_recv,
    a_send,
    a_recv,
    b_send,
    b_recv,
    c_send,
    c_recv,
):
    layers, channels, width = w_ref.shape
    pixels = cp_ref.shape[-1]
    half = channels // 2
    step_size = 1.0 / (layers * depth)
    hops = []
    while 2 ** len(hops) < depth:
        hops.append(2 ** len(hops))
    rounds = len(hops)
    me = lax.axis_index("depth")
    lane = lax.axis_index("dp")
    side = lane % 2
    sibling = lane + 1 - 2 * side
    across = (lane + 2) % dp

    barrier = pltpu.get_barrier_semaphore()
    count = 2
    for mate in (sibling, across):
        pl.semaphore_signal(barrier, inc=1, device_id={"dp": mate}, device_id_type=MESH)
    for hop in hops:
        ahead, behind = me + hop < depth, me >= hop
        count = count + jnp.where(ahead, 1, 0) + jnp.where(behind, 1, 0)

        @pl.when(ahead)
        def _():
            pl.semaphore_signal(barrier, inc=1, device_id={"depth": me + hop}, device_id_type=MESH)

        @pl.when(behind)
        def _():
            pl.semaphore_signal(barrier, inc=1, device_id={"depth": me - hop}, device_id_type=MESH)

    pixel = lax.broadcasted_iota(jnp.int32, (1, pixels), 1)
    row, column = pixel // WID, pixel % WID
    masks = []
    for a, b in TAP_OFFSETS:
        ok = (row + a >= 0) & (row + a < pixels // WID) & (column + b >= 0) & (column + b < WID)
        masks.append(jnp.broadcast_to(ok, (channels, pixels)))

    def unfold(values, ref):
        for t, (a, b) in enumerate(TAP_OFFSETS):
            off = a * WID + b
            moved = values
            if off:
                moved = jnp.where(masks[t], pltpu.roll(values, (-off) % pixels, 1), 0.0)
            ref[t * channels : (t + 1) * channels, :] = moved.astype(jnp.bfloat16)

    def forward_layer(u, layer, which):
        squashed = jnp.tanh(u)
        slopes[which, layer] = 1.0 - squashed * squashed
        unfold(squashed, patches.at[which, layer])
        mixed = jnp.dot(
            w_ref[layer], patches[which, layer], preferred_element_type=jnp.float32
        )
        return u + step_size * mixed

    def backward_layer(g, layer, which):
        scaled = step_size * g
        rounded = scaled.astype(jnp.bfloat16)
        unfold(rounded.astype(jnp.float32), back_patches)
        grads = lax.dot_general(
            rounded,
            patches[which, layer],
            (((1,), (1,)), ((), ())),
            preferred_element_type=jnp.float32,
        )
        spread = jnp.dot(turned[layer], back_patches[...], preferred_element_type=jnp.float32)
        return g + slopes[which, layer] * spread, grads

    def along(src, dst, send, recv, target):
        return pltpu.make_async_remote_copy(
            src_ref=src,
            dst_ref=dst,
            send_sem=send,
            recv_sem=recv,
            device_id=target,
            device_id_type=MESH,
        )

    def gain_copy(r):
        return along(
            gains.at[r], gains_in.at[r], gain_send.at[r], gain_recv.at[r], {"depth": me + hops[r]}
        )

    def adj_copy(r):
        return along(
            adj_out.at[r], adj_in.at[r], adj_send.at[r], adj_recv.at[r], {"depth": me - hops[r]}
        )

    def fwd_copy(r):
        return along(
            fwd.at[r], fwd_in.at[r], fwd_send.at[r], fwd_recv.at[r], {"depth": me + hops[r]}
        )

    def relaxed_copy():
        return along(relaxed_buf, start_buf, edge_send.at[0], edge_recv.at[0], {"depth": me + 1})

    def back_copy():
        return along(back_buf, bar_buf, edge_send.at[1], edge_recv.at[1], {"depth": me - 1})

    eye = lax.broadcasted_iota(jnp.int32, (channels, channels), 0) == lax.broadcasted_iota(
        jnp.int32, (channels, channels), 1
    )

    def gain_column(r):
        line = jnp.broadcast_to(gains[r, 0:1, 0:channels], (channels, channels))
        return jnp.sum(jnp.where(eye, line, 0.0), axis=1, keepdims=True)

    def start_adj(r):
        @pl.when(me >= hops[r])
        def _():
            adj_out[r] = gain_column(r) * (cot_ref[0, 0] + passed_buf[...])
            adj_copy(r).start()

    def take_gain(r):
        @pl.when(me >= hops[r])
        def _():
            gain_copy(r).wait_recv()
            gains[r + 1] = gains[r] * gains_in[r]

        @pl.when(me < hops[r])
        def _():
            gains[r + 1] = gains[r]

    def start_gain(r):
        @pl.when(me + hops[r] < depth)
        def _():
            gain_copy(r).start()

    def take_adj(r):
        @pl.when(me + hops[r] < depth)
        def _():
            adj_copy(r).wait_recv()
            passed_buf[...] = passed_buf[...] + adj_in[r]

    def start_fwd(r):
        @pl.when(me + hops[r] < depth)
        def _():
            fwd_copy(r).start()

    def take_fwd(r):
        @pl.when(me >= hops[r])
        def _():
            fwd_copy(r).wait_recv()
            fwd[r + 1] = fwd[r] + gain_column(r) * fwd_in[r]

        @pl.when(me < hops[r])
        def _():
            fwd[r + 1] = fwd[r]

    gains[0] = jnp.zeros_like(gains[0])
    gains[0, 0:1, 0:channels] = gain_ref[...]
    passed_buf[...] = jnp.zeros_like(passed_buf)
    own = cp_ref[0, 0]
    u = forward_layer(own, 0, 0)
    pl.semaphore_wait(barrier, count)
    start_adj(0)
    if rounds > 1:
        start_gain(0)
    for layer in range(1, layers):
        u = forward_layer(u, layer, 0)
    relaxed_buf[...] = u

    @pl.when(me + 1 < depth)
    def _():
        relaxed_copy().start()

    for r in range(rounds - 1):
        take_gain(r)
        if r + 1 < rounds - 1:
            start_gain(r + 1)
        take_adj(r)
        start_adj(r + 1)

    one = jnp.where(eye, 1.0, 0.0).astype(jnp.bfloat16)
    for layer in range(layers):
        pieces = []
        for t in reversed(range(len(TAP_OFFSETS))):
            block = w_ref[layer, :, t * channels : (t + 1) * channels]
            pieces.append(
                lax.dot_general(
                    one, block, (((1,), (1,)), ((), ())), preferred_element_type=jnp.float32
                ).astype(jnp.bfloat16)
            )
        turned[layer] = jnp.concatenate(pieces, axis=1)

    @pl.when(me > 0)
    def _():
        relaxed_back = along(
            relaxed_buf, start_buf, edge_send.at[0], edge_recv.at[0], {"depth": me - 1}
        )
        relaxed_back.wait_recv()

    @pl.when(me == 0)
    def _():
        start_buf[...] = own

    u = start_buf[...]
    for layer in range(layers):
        u = forward_layer(u, layer, 1)
    fwd[0] = u - jnp.where(me == 0, 0.0, 1.0) * gain_column(0) * start_buf[...]
    start_fwd(0)
    take_adj(rounds - 1)

    g = cot_ref[0, 0] + passed_buf[...]
    for position, layer in enumerate(reversed(range(layers))):
        g, grads = backward_layer(g, layer, 1)
        start_grads[layer] = grads
    back_buf[...] = g

    @pl.when(me > 0)
    def _():
        back_copy().start()

    for r in range(rounds):
        take_fwd(r)
        if r + 1 < rounds:
            start_fwd(r + 1)
    corr_ref[0, 0] = fwd[rounds]

    @pl.when(me + 1 < depth)
    def _():
        back_copy().wait_recv()

    @pl.when(me + 1 == depth)
    def _():
        bar_buf[...] = jnp.zeros_like(bar_buf)

    g = bar_buf[...] - passed_buf[...]

    mine = pl.ds(pl.multiple_of(side * half, half), half)
    other = pl.ds(pl.multiple_of((1 - side) * half, half), half)

    def a_copy(layer):
        return along(
            start_grads.at[layer, other],
            part_a.at[layer],
            a_send.at[layer],
            a_recv.at[layer],
            {"dp": sibling},
        )

    def b_copy(layer):
        return along(
            sum_a.at[layer], part_b.at[layer], b_send.at[layer], b_recv.at[layer], {"dp": across}
        )

    def c_copy(layer):
        return along(
            sum_b.at[layer],
            gw_ref.at[layer, mine],
            c_send.at[layer],
            c_recv.at[layer],
            {"dp": sibling},
        )

    def middle(layer):
        a_copy(layer).wait_recv()
        sum_a[layer] = start_grads[layer, mine, :] + part_a[layer]
        b_copy(layer).start()

    def last(layer):
        b_copy(layer).wait_recv()
        sum_b[layer] = sum_a[layer] + part_b[layer]
        c_copy(layer).start()
        gw_ref[layer, mine, :] = sum_b[layer]

    for layer in reversed(range(layers)):
        g, grads = backward_layer(g, layer, 0)
        start_grads[layer] = start_grads[layer] + grads
        a_copy(layer).start()
        if layer + 1 < layers:
            middle(layer + 1)
    gcp_ref[0, 0] = g + jnp.where(me == 0, 1.0, 0.0) * back_buf[...]
    middle(0)
    for layer in reversed(range(layers)):
        last(layer)
    for layer in reversed(range(layers)):
        c_copy(layer).wait_recv()
        a_copy(layer).wait_send()
        b_copy(layer).wait_send()
        c_copy(layer).wait_send()

    for r in range(rounds):
        if r + 1 < rounds:

            @pl.when(me + hops[r] < depth)
            def _():
                gain_copy(r).wait_send()

        @pl.when(me >= hops[r])
        def _():
            adj_copy(r).wait_send()

        @pl.when(me + hops[r] < depth)
        def _():
            fwd_copy(r).wait_send()

    @pl.when(me + 1 < depth)
    def _():
        relaxed_copy().wait_send()

    @pl.when(me > 0)
    def _():
        back_copy().wait_send()


def solution(mesh):
    depth, dp = mesh.shape["depth"], mesh.shape["dp"]
    rounds = max(1, (depth - 1).bit_length())

    def step(cpoints, weights, coarse_gain, cotangent):
        layers, channels, width = weights.shape
        pixels = cpoints.shape[-1]
        state = (channels, pixels)
        half = (layers, channels // 2, width)
        f32, bf16 = jnp.float32, jnp.bfloat16
        dma = pltpu.SemaphoreType.DMA
        vmem = pl.BlockSpec(memory_space=pltpu.VMEM)
        return pl.pallas_call(
            functools.partial(kernel, depth, dp),
            out_shape=(
                jax.ShapeDtypeStruct(cpoints.shape, f32),
                jax.ShapeDtypeStruct(cpoints.shape, f32),
                jax.ShapeDtypeStruct(weights.shape, f32),
            ),
            in_specs=[vmem] * 4,
            out_specs=(vmem,) * 3,
            scratch_shapes=[
                pltpu.VMEM((2, layers, width, pixels), bf16),
                pltpu.VMEM((2, layers) + state, f32),
                pltpu.VMEM((width, pixels), bf16),
                pltpu.VMEM((layers, channels, width), bf16),
                pltpu.VMEM((layers, channels, width), f32),
                pltpu.VMEM(state, f32),
                pltpu.VMEM(state, f32),
                pltpu.VMEM(state, f32),
                pltpu.VMEM(state, f32),
                pltpu.VMEM(state, f32),
                pltpu.VMEM((rounds, 8, 128), f32),
                pltpu.VMEM((rounds, 8, 128), f32),
                pltpu.VMEM((rounds,) + state, f32),
                pltpu.VMEM((rounds,) + state, f32),
                pltpu.VMEM((rounds + 1,) + state, f32),
                pltpu.VMEM((rounds,) + state, f32),
                pltpu.VMEM(half, f32),
                pltpu.VMEM(half, f32),
                pltpu.VMEM(half, f32),
                pltpu.VMEM(half, f32),
                dma((rounds,)),
                dma((rounds,)),
                dma((rounds,)),
                dma((rounds,)),
                dma((rounds,)),
                dma((rounds,)),
                dma((2,)),
                dma((2,)),
                dma((layers,)),
                dma((layers,)),
                dma((layers,)),
                dma((layers,)),
                dma((layers,)),
                dma((layers,)),
            ],
            compiler_params=pltpu.CompilerParams(
                collective_id=0, has_side_effects=True, vmem_limit_bytes=40 * 1024 * 1024
            ),
        )(cpoints, weights, coarse_gain, cotangent)

    states = P("depth", "dp", None, None)
    blocks = P("depth", None, None)
    return jax.shard_map(
        step,
        mesh=mesh,
        in_specs=(states, blocks, P("depth", None), states),
        out_specs=(states, states, blocks),
        check_vma=False,
    )
```

```python
import functools

import jax
import jax.numpy as jnp
from jax import lax
from jax.experimental import pallas as pl
from jax.experimental.pallas import tpu as pltpu
from jax.sharding import PartitionSpec as P

MESH = pl.DeviceIdType.MESH
WID = 16
TAP_OFFSETS = [(-1, -1), (-1, 0), (-1, 1), (0, -1), (0, 0), (0, 1), (1, -1), (1, 0), (1, 1)]


def kernel(
    depth,
    dp,
    cp_hbm,
    w_hbm,
    gain_hbm,
    cot_hbm,
    corr_ref,
    gcp_ref,
    gw_ref,
    cp_ref,
    w_ref,
    gain_ref,
    cot_ref,
    in_sem,
    out_sem,
    gcp_buf,
    patches,
    slopes,
    back_patches,
    turned,
    start_grads,
    relaxed_buf,
    start_buf,
    back_buf,
    bar_buf,
    passed_buf,
    gains,
    gains_in,
    adj_out,
    adj_in,
    fwd,
    fwd_in,
    sum_a,
    sum_b,
    part_a,
    part_b,
    gain_send,
    gain_recv,
    adj_send,
    adj_recv,
    fwd_send,
    fwd_recv,
    edge_send,
    edge_recv,
    a_send,
    a_recv,
    b_send,
    b_recv,
    c_send,
    c_recv,
):
    layers, channels, width = w_ref.shape
    pixels = cp_ref.shape[-1]
    fetches = [
        pltpu.make_async_copy(cp_hbm, cp_ref, in_sem.at[0]),
        pltpu.make_async_copy(gain_hbm, gain_ref, in_sem.at[1]),
        pltpu.make_async_copy(cot_hbm, cot_ref, in_sem.at[2]),
    ]
    for layer in range(layers):
        fetches.append(
            pltpu.make_async_copy(w_hbm.at[layer], w_ref.at[layer], in_sem.at[3 + layer])
        )
    for fetch in fetches:
        fetch.start()
    half = channels // 2
    step_size = 1.0 / (layers * depth)
    hops = []
    while 2 ** len(hops) < depth:
        hops.append(2 ** len(hops))
    rounds = len(hops)
    me = lax.axis_index("depth")
    lane = lax.axis_index("dp")
    side = lane % 2
    sibling = lane + 1 - 2 * side
    across = (lane + 2) % dp

    barrier = pltpu.get_barrier_semaphore()
    count = 2
    for mate in (sibling, across):
        pl.semaphore_signal(barrier, inc=1, device_id={"dp": mate}, device_id_type=MESH)
    for hop in hops:
        ahead, behind = me + hop < depth, me >= hop
        count = count + jnp.where(ahead, 1, 0) + jnp.where(behind, 1, 0)

        @pl.when(ahead)
        def _():
            pl.semaphore_signal(barrier, inc=1, device_id={"depth": me + hop}, device_id_type=MESH)

        @pl.when(behind)
        def _():
            pl.semaphore_signal(barrier, inc=1, device_id={"depth": me - hop}, device_id_type=MESH)

    pixel = lax.broadcasted_iota(jnp.int32, (8, pixels), 1)
    row, column = pixel // WID, pixel % WID
    masks = []
    for a, b in TAP_OFFSETS:
        ok = (row + a >= 0) & (row + a < pixels // WID) & (column + b >= 0) & (column + b < WID)
        masks.append(jnp.where(ok, 1.0, 0.0)[None])

    def unfold(values, ref):
        for t, (a, b) in enumerate(TAP_OFFSETS):
            off = a * WID + b
            moved = values
            if off:
                moved = pltpu.roll(values, (-off) % pixels, 1).reshape(channels // 8, 8, pixels)
                moved = (moved * masks[t]).reshape(channels, pixels)
            ref[t * channels : (t + 1) * channels, :] = moved.astype(jnp.bfloat16)

    def forward_layer(u, layer, which):
        squashed = jnp.tanh(u)
        slopes[which, layer] = 1.0 - squashed * squashed
        unfold(squashed, patches.at[which, layer])
        mixed = jnp.dot(
            w_ref[layer], patches[which, layer], preferred_element_type=jnp.float32
        )
        return u + step_size * mixed

    def backward_layer(g, layer, which):
        scaled = step_size * g
        rounded = scaled.astype(jnp.bfloat16)
        unfold(rounded.astype(jnp.float32), back_patches)
        grads = lax.dot_general(
            rounded,
            patches[which, layer],
            (((1,), (1,)), ((), ())),
            preferred_element_type=jnp.float32,
        )
        spread = jnp.dot(turned[layer], back_patches[...], preferred_element_type=jnp.float32)
        return g + slopes[which, layer] * spread, grads

    def along(src, dst, send, recv, target):
        return pltpu.make_async_remote_copy(
            src_ref=src,
            dst_ref=dst,
            send_sem=send,
            recv_sem=recv,
            device_id=target,
            device_id_type=MESH,
        )

    def gain_copy(r):
        return along(
            gains.at[r], gains_in.at[r], gain_send.at[r], gain_recv.at[r], {"depth": me + hops[r]}
        )

    def adj_copy(r):
        return along(
            adj_out.at[r], adj_in.at[r], adj_send.at[r], adj_recv.at[r], {"depth": me - hops[r]}
        )

    def fwd_copy(r):
        return along(
            fwd.at[r], fwd_in.at[r], fwd_send.at[r], fwd_recv.at[r], {"depth": me + hops[r]}
        )

    def relaxed_copy():
        return along(relaxed_buf, start_buf, edge_send.at[0], edge_recv.at[0], {"depth": me + 1})

    def back_copy():
        return along(back_buf, bar_buf, edge_send.at[1], edge_recv.at[1], {"depth": me - 1})

    eye = lax.broadcasted_iota(jnp.int32, (channels, channels), 0) == lax.broadcasted_iota(
        jnp.int32, (channels, channels), 1
    )

    def gain_column(r):
        line = jnp.broadcast_to(gains[r, 0:1, 0:channels], (channels, channels))
        return jnp.sum(jnp.where(eye, line, 0.0), axis=1, keepdims=True)

    def start_adj(r):
        @pl.when(me >= hops[r])
        def _():
            adj_out[r] = gain_column(r) * (cot_ref[0, 0] + passed_buf[...])
            adj_copy(r).start()

    def take_gain(r):
        @pl.when(me >= hops[r])
        def _():
            gain_copy(r).wait_recv()
            gains[r + 1] = gains[r] * gains_in[r]

        @pl.when(me < hops[r])
        def _():
            gains[r + 1] = gains[r]

    def start_gain(r):
        @pl.when(me + hops[r] < depth)
        def _():
            gain_copy(r).start()

    def take_adj(r):
        @pl.when(me + hops[r] < depth)
        def _():
            adj_copy(r).wait_recv()
            passed_buf[...] = passed_buf[...] + adj_in[r]

    def start_fwd(r):
        @pl.when(me + hops[r] < depth)
        def _():
            fwd_copy(r).start()

    def take_fwd(r):
        @pl.when(me >= hops[r])
        def _():
            fwd_copy(r).wait_recv()
            fwd[r + 1] = fwd[r] + gain_column(r) * fwd_in[r]

        @pl.when(me < hops[r])
        def _():
            fwd[r + 1] = fwd[r]

    gains[0] = jnp.zeros_like(gains[0])
    fetches[1].wait()
    gains[0, 0:1, 0:channels] = gain_ref[...]
    passed_buf[...] = jnp.zeros_like(passed_buf)
    fetches[0].wait()
    own = cp_ref[0, 0]
    fetches[3].wait()
    u = forward_layer(own, 0, 0)
    pl.semaphore_wait(barrier, count)
    fetches[2].wait()
    start_adj(0)
    if rounds > 1:
        start_gain(0)
    for layer in range(1, layers):
        fetches[3 + layer].wait()
        u = forward_layer(u, layer, 0)
    relaxed_buf[...] = u

    @pl.when(me + 1 < depth)
    def _():
        relaxed_copy().start()

    for r in range(rounds - 1):
        take_gain(r)
        if r + 1 < rounds - 1:
            start_gain(r + 1)
        take_adj(r)
        start_adj(r + 1)

    one = jnp.where(eye, 1.0, 0.0).astype(jnp.bfloat16)
    for layer in range(layers):
        pieces = []
        for t in reversed(range(len(TAP_OFFSETS))):
            block = w_ref[layer, :, t * channels : (t + 1) * channels]
            pieces.append(
                lax.dot_general(
                    one, block, (((1,), (1,)), ((), ())), preferred_element_type=jnp.float32
                ).astype(jnp.bfloat16)
            )
        turned[layer] = jnp.concatenate(pieces, axis=1)

    @pl.when(me > 0)
    def _():
        relaxed_back = along(
            relaxed_buf, start_buf, edge_send.at[0], edge_recv.at[0], {"depth": me - 1}
        )
        relaxed_back.wait_recv()

    @pl.when(me == 0)
    def _():
        start_buf[...] = own

    u = start_buf[...]
    for layer in range(layers):
        u = forward_layer(u, layer, 1)
    fwd[0] = u - jnp.where(me == 0, 0.0, 1.0) * gain_column(0) * start_buf[...]
    start_fwd(0)
    take_adj(rounds - 1)

    g = cot_ref[0, 0] + passed_buf[...]
    for position, layer in enumerate(reversed(range(layers))):
        g, grads = backward_layer(g, layer, 1)
        start_grads[layer] = grads
    back_buf[...] = g

    @pl.when(me > 0)
    def _():
        back_copy().start()

    for r in range(rounds):
        take_fwd(r)
        if r + 1 < rounds:
            start_fwd(r + 1)
    put_corr = pltpu.make_async_copy(fwd.at[rounds], corr_ref.at[0, 0], out_sem.at[0])
    put_corr.start()

    @pl.when(me + 1 < depth)
    def _():
        back_copy().wait_recv()

    @pl.when(me + 1 == depth)
    def _():
        bar_buf[...] = jnp.zeros_like(bar_buf)

    g = bar_buf[...] - passed_buf[...]

    mine = pl.ds(pl.multiple_of(side * half, half), half)
    other = pl.ds(pl.multiple_of((1 - side) * half, half), half)

    def a_copy(layer):
        return along(
            start_grads.at[layer, other],
            part_a.at[layer],
            a_send.at[layer],
            a_recv.at[layer],
            {"dp": sibling},
        )

    def b_copy(layer):
        return along(
            sum_a.at[layer], part_b.at[layer], b_send.at[layer], b_recv.at[layer], {"dp": across}
        )

    def c_copy(layer):
        return along(
            sum_b.at[layer],
            gw_ref.at[layer, mine],
            c_send.at[layer],
            c_recv.at[layer],
            {"dp": sibling},
        )

    def middle(layer):
        a_copy(layer).wait_recv()
        sum_a[layer] = start_grads[layer, mine, :] + part_a[layer]
        b_copy(layer).start()

    def last(layer):
        b_copy(layer).wait_recv()
        sum_b[layer] = sum_a[layer] + part_b[layer]
        c_copy(layer).start()
        put_own(layer).start()

    def put_own(layer):
        return pltpu.make_async_copy(
            sum_b.at[layer], gw_ref.at[layer, mine], out_sem.at[2 + layer]
        )

    for layer in reversed(range(layers)):
        g, grads = backward_layer(g, layer, 0)
        start_grads[layer] = start_grads[layer] + grads
        a_copy(layer).start()
        if layer + 1 < layers:
            middle(layer + 1)
    gcp_buf[...] = g + jnp.where(me == 0, 1.0, 0.0) * back_buf[...]
    put_gcp = pltpu.make_async_copy(gcp_buf, gcp_ref.at[0, 0], out_sem.at[1])
    put_gcp.start()
    middle(0)
    for layer in reversed(range(layers)):
        last(layer)
    for layer in reversed(range(layers)):
        c_copy(layer).wait_recv()
        put_own(layer).wait()
        a_copy(layer).wait_send()
        b_copy(layer).wait_send()
        c_copy(layer).wait_send()

    put_corr.wait()
    put_gcp.wait()
    for r in range(rounds):
        if r + 1 < rounds:

            @pl.when(me + hops[r] < depth)
            def _():
                gain_copy(r).wait_send()

        @pl.when(me >= hops[r])
        def _():
            adj_copy(r).wait_send()

        @pl.when(me + hops[r] < depth)
        def _():
            fwd_copy(r).wait_send()

    @pl.when(me + 1 < depth)
    def _():
        relaxed_copy().wait_send()

    @pl.when(me > 0)
    def _():
        back_copy().wait_send()


def deliver(corr_in, gcp_in, gw_in, corr_out, gcp_out, gw_out, sem):
    moves = [
        pltpu.make_async_copy(corr_in, corr_out, sem.at[0]),
        pltpu.make_async_copy(gcp_in, gcp_out, sem.at[1]),
    ]
    for layer in range(gw_in.shape[0]):
        moves.append(
            pltpu.make_async_copy(gw_in.at[layer], gw_out.at[layer], sem.at[2 + layer])
        )
    for move in moves:
        move.start()
    for move in moves:
        move.wait()


def solution(mesh):
    depth, dp = mesh.shape["depth"], mesh.shape["dp"]
    rounds = max(1, (depth - 1).bit_length())

    def step(cpoints, weights, coarse_gain, cotangent):
        layers, channels, width = weights.shape
        pixels = cpoints.shape[-1]
        state = (channels, pixels)
        half = (layers, channels // 2, width)
        f32, bf16 = jnp.float32, jnp.bfloat16
        dma = pltpu.SemaphoreType.DMA
        hbm = pl.BlockSpec(memory_space=pltpu.HBM)
        results = (
            jax.ShapeDtypeStruct(cpoints.shape, f32),
            jax.ShapeDtypeStruct(cpoints.shape, f32),
            jax.ShapeDtypeStruct(weights.shape, f32),
        )
        found = pl.pallas_call(
            functools.partial(kernel, depth, dp),
            out_shape=results,
            in_specs=[hbm] * 4,
            out_specs=(hbm,) * 3,
            scratch_shapes=[
                pltpu.VMEM(cpoints.shape, f32),
                pltpu.VMEM(weights.shape, bf16),
                pltpu.VMEM(coarse_gain.shape, f32),
                pltpu.VMEM(cotangent.shape, f32),
                dma((3 + layers,)),
                dma((2 + layers,)),
                pltpu.VMEM(state, f32),
                pltpu.VMEM((2, layers, width, pixels), bf16),
                pltpu.VMEM((2, layers) + state, f32),
                pltpu.VMEM((width, pixels), bf16),
                pltpu.VMEM((layers, channels, width), bf16),
                pltpu.VMEM((layers, channels, width), f32),
                pltpu.VMEM(state, f32),
                pltpu.VMEM(state, f32),
                pltpu.VMEM(state, f32),
                pltpu.VMEM(state, f32),
                pltpu.VMEM(state, f32),
                pltpu.VMEM((rounds, 8, 128), f32),
                pltpu.VMEM((rounds, 8, 128), f32),
                pltpu.VMEM((rounds,) + state, f32),
                pltpu.VMEM((rounds,) + state, f32),
                pltpu.VMEM((rounds + 1,) + state, f32),
                pltpu.VMEM((rounds,) + state, f32),
                pltpu.VMEM(half, f32),
                pltpu.VMEM(half, f32),
                pltpu.VMEM(half, f32),
                pltpu.VMEM(half, f32),
                dma((rounds,)),
                dma((rounds,)),
                dma((rounds,)),
                dma((rounds,)),
                dma((rounds,)),
                dma((rounds,)),
                dma((2,)),
                dma((2,)),
                dma((layers,)),
                dma((layers,)),
                dma((layers,)),
                dma((layers,)),
                dma((layers,)),
                dma((layers,)),
            ],
            compiler_params=pltpu.CompilerParams(
                collective_id=0, has_side_effects=True, vmem_limit_bytes=60 * 1024 * 1024
            ),
        )(cpoints, weights, coarse_gain, cotangent)
        return pl.pallas_call(
            deliver,
            out_shape=results,
            in_specs=[hbm] * 3,
            out_specs=(hbm,) * 3,
            scratch_shapes=[dma((2 + layers,))],
            compiler_params=pltpu.CompilerParams(vmem_limit_bytes=60 * 1024 * 1024),
        )(*found)

    states = P("depth", "dp", None, None)
    blocks = P("depth", None, None)
    return jax.shard_map(
        step,
        mesh=mesh,
        in_specs=(states, blocks, P("depth", None), states),
        out_specs=(states, states, blocks),
        check_vma=False,
    )
```

```python
import functools

import jax
import jax.numpy as jnp
from jax import lax
from jax.experimental import pallas as pl
from jax.experimental.pallas import tpu as pltpu
from jax.sharding import PartitionSpec as P

MESH = pl.DeviceIdType.MESH
WID = 16
TAP_OFFSETS = [(-1, -1), (-1, 0), (-1, 1), (0, -1), (0, 0), (0, 1), (1, -1), (1, 0), (1, 1)]


def kernel(
    depth,
    dp,
    cp_hbm,
    w_hbm,
    gain_hbm,
    cot_hbm,
    corr_ref,
    gcp_ref,
    gw_ref,
    cp_ref,
    w_ref,
    gain_ref,
    cot_ref,
    in_sem,
    patches,
    slopes,
    back_patches,
    turned,
    start_grads,
    relaxed_buf,
    start_buf,
    back_buf,
    bar_buf,
    passed_buf,
    gains,
    gains_in,
    adj_out,
    adj_in,
    fwd,
    fwd_in,
    sum_a,
    sum_b,
    part_a,
    part_b,
    gain_send,
    gain_recv,
    adj_send,
    adj_recv,
    fwd_send,
    fwd_recv,
    edge_send,
    edge_recv,
    a_send,
    a_recv,
    b_send,
    b_recv,
    c_send,
    c_recv,
):
    layers, channels, width = w_ref.shape
    pixels = cp_ref.shape[-1]
    fetches = [
        pltpu.make_async_copy(cp_hbm, cp_ref, in_sem.at[0]),
        pltpu.make_async_copy(gain_hbm, gain_ref, in_sem.at[1]),
        pltpu.make_async_copy(cot_hbm, cot_ref, in_sem.at[2]),
    ]
    for layer in range(layers):
        fetches.append(
            pltpu.make_async_copy(w_hbm.at[layer], w_ref.at[layer], in_sem.at[3 + layer])
        )
    for fetch in fetches:
        fetch.start()
    half = channels // 2
    step_size = 1.0 / (layers * depth)
    hops = []
    while 2 ** len(hops) < depth:
        hops.append(2 ** len(hops))
    rounds = len(hops)
    me = lax.axis_index("depth")
    lane = lax.axis_index("dp")
    side = lane % 2
    sibling = lane + 1 - 2 * side
    across = (lane + 2) % dp

    barrier = pltpu.get_barrier_semaphore()
    count = 2
    for mate in (sibling, across):
        pl.semaphore_signal(barrier, inc=1, device_id={"dp": mate}, device_id_type=MESH)
    for hop in hops:
        ahead, behind = me + hop < depth, me >= hop
        count = count + jnp.where(ahead, 1, 0) + jnp.where(behind, 1, 0)

        @pl.when(ahead)
        def _():
            pl.semaphore_signal(barrier, inc=1, device_id={"depth": me + hop}, device_id_type=MESH)

        @pl.when(behind)
        def _():
            pl.semaphore_signal(barrier, inc=1, device_id={"depth": me - hop}, device_id_type=MESH)

    pixel = lax.broadcasted_iota(jnp.int32, (8, pixels), 1)
    row, column = pixel // WID, pixel % WID
    masks = []
    for a, b in TAP_OFFSETS:
        ok = (row + a >= 0) & (row + a < pixels // WID) & (column + b >= 0) & (column + b < WID)
        masks.append(jnp.where(ok, 1.0, 0.0)[None])

    def unfold(values, ref):
        for t, (a, b) in enumerate(TAP_OFFSETS):
            off = a * WID + b
            moved = values
            if off:
                moved = pltpu.roll(values, (-off) % pixels, 1).reshape(channels // 8, 8, pixels)
                moved = (moved * masks[t]).reshape(channels, pixels)
            ref[t * channels : (t + 1) * channels, :] = moved.astype(jnp.bfloat16)

    def forward_layer(u, layer, which):
        squashed = jnp.tanh(u)
        slopes[which, layer] = 1.0 - squashed * squashed
        unfold(squashed, patches.at[which, layer])
        mixed = jnp.dot(
            w_ref[layer], patches[which, layer], preferred_element_type=jnp.float32
        )
        return u + step_size * mixed

    def backward_layer(g, layer, which):
        scaled = step_size * g
        rounded = scaled.astype(jnp.bfloat16)
        unfold(rounded.astype(jnp.float32), back_patches)
        grads = lax.dot_general(
            rounded,
            patches[which, layer],
            (((1,), (1,)), ((), ())),
            preferred_element_type=jnp.float32,
        )
        spread = jnp.dot(turned[layer], back_patches[...], preferred_element_type=jnp.float32)
        return g + slopes[which, layer] * spread, grads

    def along(src, dst, send, recv, target):
        return pltpu.make_async_remote_copy(
            src_ref=src,
            dst_ref=dst,
            send_sem=send,
            recv_sem=recv,
            device_id=target,
            device_id_type=MESH,
        )

    def gain_copy(r):
        return along(
            gains.at[r], gains_in.at[r], gain_send.at[r], gain_recv.at[r], {"depth": me + hops[r]}
        )

    def adj_copy(r):
        return along(
            adj_out.at[r], adj_in.at[r], adj_send.at[r], adj_recv.at[r], {"depth": me - hops[r]}
        )

    def fwd_copy(r):
        return along(
            fwd.at[r], fwd_in.at[r], fwd_send.at[r], fwd_recv.at[r], {"depth": me + hops[r]}
        )

    def relaxed_copy():
        return along(relaxed_buf, start_buf, edge_send.at[0], edge_recv.at[0], {"depth": me + 1})

    def back_copy():
        return along(back_buf, bar_buf, edge_send.at[1], edge_recv.at[1], {"depth": me - 1})

    eye = lax.broadcasted_iota(jnp.int32, (channels, channels), 0) == lax.broadcasted_iota(
        jnp.int32, (channels, channels), 1
    )

    def gain_column(r):
        line = jnp.broadcast_to(gains[r, 0:1, 0:channels], (channels, channels))
        return jnp.sum(jnp.where(eye, line, 0.0), axis=1, keepdims=True)

    def start_adj(r):
        @pl.when(me >= hops[r])
        def _():
            adj_out[r] = gain_column(r) * (cot_ref[0, 0] + passed_buf[...])
            adj_copy(r).start()

    def take_gain(r):
        @pl.when(me >= hops[r])
        def _():
            gain_copy(r).wait_recv()
            gains[r + 1] = gains[r] * gains_in[r]

        @pl.when(me < hops[r])
        def _():
            gains[r + 1] = gains[r]

    def start_gain(r):
        @pl.when(me + hops[r] < depth)
        def _():
            gain_copy(r).start()

    def take_adj(r):
        @pl.when(me + hops[r] < depth)
        def _():
            adj_copy(r).wait_recv()
            passed_buf[...] = passed_buf[...] + adj_in[r]

    def start_fwd(r):
        @pl.when(me + hops[r] < depth)
        def _():
            fwd_copy(r).start()

    def take_fwd(r):
        @pl.when(me >= hops[r])
        def _():
            fwd_copy(r).wait_recv()
            fwd[r + 1] = fwd[r] + gain_column(r) * fwd_in[r]

        @pl.when(me < hops[r])
        def _():
            fwd[r + 1] = fwd[r]

    gains[0] = jnp.zeros_like(gains[0])
    fetches[1].wait()
    gains[0, 0:1, 0:channels] = gain_ref[...]
    passed_buf[...] = jnp.zeros_like(passed_buf)
    fetches[0].wait()
    own = cp_ref[0, 0]
    fetches[3].wait()
    u = forward_layer(own, 0, 0)
    pl.semaphore_wait(barrier, count)
    fetches[2].wait()
    start_adj(0)
    if rounds > 1:
        start_gain(0)
    for layer in range(1, layers):
        fetches[3 + layer].wait()
        u = forward_layer(u, layer, 0)
    relaxed_buf[...] = u

    @pl.when(me + 1 < depth)
    def _():
        relaxed_copy().start()

    for r in range(rounds - 1):
        take_gain(r)
        if r + 1 < rounds - 1:
            start_gain(r + 1)
        take_adj(r)
        start_adj(r + 1)

    one = jnp.where(eye, 1.0, 0.0).astype(jnp.bfloat16)
    for layer in range(layers):
        pieces = []
        for t in reversed(range(len(TAP_OFFSETS))):
            block = w_ref[layer, :, t * channels : (t + 1) * channels]
            pieces.append(
                lax.dot_general(
                    one, block, (((1,), (1,)), ((), ())), preferred_element_type=jnp.float32
                ).astype(jnp.bfloat16)
            )
        turned[layer] = jnp.concatenate(pieces, axis=1)

    @pl.when(me > 0)
    def _():
        relaxed_back = along(
            relaxed_buf, start_buf, edge_send.at[0], edge_recv.at[0], {"depth": me - 1}
        )
        relaxed_back.wait_recv()

    @pl.when(me == 0)
    def _():
        start_buf[...] = own

    u = start_buf[...]
    for layer in range(layers):
        u = forward_layer(u, layer, 1)
    fwd[0] = u - jnp.where(me == 0, 0.0, 1.0) * gain_column(0) * start_buf[...]
    start_fwd(0)
    take_adj(rounds - 1)

    g = cot_ref[0, 0] + passed_buf[...]
    for position, layer in enumerate(reversed(range(layers))):
        g, grads = backward_layer(g, layer, 1)
        start_grads[layer] = grads
    back_buf[...] = g

    @pl.when(me > 0)
    def _():
        back_copy().start()

    for r in range(rounds):
        take_fwd(r)
        if r + 1 < rounds:
            start_fwd(r + 1)
    corr_ref[0, 0] = fwd[rounds]

    @pl.when(me + 1 < depth)
    def _():
        back_copy().wait_recv()

    @pl.when(me + 1 == depth)
    def _():
        bar_buf[...] = jnp.zeros_like(bar_buf)

    g = bar_buf[...] - passed_buf[...]

    mine = pl.ds(pl.multiple_of(side * half, half), half)
    other = pl.ds(pl.multiple_of((1 - side) * half, half), half)

    def a_copy(layer):
        return along(
            start_grads.at[layer, other],
            part_a.at[layer],
            a_send.at[layer],
            a_recv.at[layer],
            {"dp": sibling},
        )

    def b_copy(layer):
        return along(
            sum_a.at[layer], part_b.at[layer], b_send.at[layer], b_recv.at[layer], {"dp": across}
        )

    def c_copy(layer):
        return along(
            sum_b.at[layer],
            gw_ref.at[layer, mine],
            c_send.at[layer],
            c_recv.at[layer],
            {"dp": sibling},
        )

    def middle(layer):
        a_copy(layer).wait_recv()
        sum_a[layer] = start_grads[layer, mine, :] + part_a[layer]
        b_copy(layer).start()

    def last(layer):
        b_copy(layer).wait_recv()
        sum_b[layer] = sum_a[layer] + part_b[layer]
        c_copy(layer).start()
        gw_ref[layer, mine, :] = sum_b[layer]

    for layer in reversed(range(layers)):
        g, grads = backward_layer(g, layer, 0)
        start_grads[layer] = start_grads[layer] + grads
        a_copy(layer).start()
        if layer + 1 < layers:
            middle(layer + 1)
    gcp_ref[0, 0] = g + jnp.where(me == 0, 1.0, 0.0) * back_buf[...]
    middle(0)
    for layer in reversed(range(layers)):
        last(layer)
    for layer in reversed(range(layers)):
        c_copy(layer).wait_recv()
        a_copy(layer).wait_send()
        b_copy(layer).wait_send()
        c_copy(layer).wait_send()

    for r in range(rounds):
        if r + 1 < rounds:

            @pl.when(me + hops[r] < depth)
            def _():
                gain_copy(r).wait_send()

        @pl.when(me >= hops[r])
        def _():
            adj_copy(r).wait_send()

        @pl.when(me + hops[r] < depth)
        def _():
            fwd_copy(r).wait_send()

    @pl.when(me + 1 < depth)
    def _():
        relaxed_copy().wait_send()

    @pl.when(me > 0)
    def _():
        back_copy().wait_send()


def deliver(corr_in, gcp_in, gw_in, corr_out, gcp_out, gw_out, sem):
    moves = [
        pltpu.make_async_copy(corr_in, corr_out, sem.at[0]),
        pltpu.make_async_copy(gcp_in, gcp_out, sem.at[1]),
    ]
    for layer in range(gw_in.shape[0]):
        moves.append(
            pltpu.make_async_copy(gw_in.at[layer], gw_out.at[layer], sem.at[2 + layer])
        )
    for move in moves:
        move.start()
    for move in moves:
        move.wait()


def solution(mesh):
    depth, dp = mesh.shape["depth"], mesh.shape["dp"]
    rounds = max(1, (depth - 1).bit_length())

    def step(cpoints, weights, coarse_gain, cotangent):
        layers, channels, width = weights.shape
        pixels = cpoints.shape[-1]
        state = (channels, pixels)
        half = (layers, channels // 2, width)
        f32, bf16 = jnp.float32, jnp.bfloat16
        dma = pltpu.SemaphoreType.DMA
        vmem = pl.BlockSpec(memory_space=pltpu.VMEM)
        hbm = pl.BlockSpec(memory_space=pltpu.HBM)
        results = (
            jax.ShapeDtypeStruct(cpoints.shape, f32),
            jax.ShapeDtypeStruct(cpoints.shape, f32),
            jax.ShapeDtypeStruct(weights.shape, f32),
        )
        found = pl.pallas_call(
            functools.partial(kernel, depth, dp),
            out_shape=results,
            in_specs=[hbm] * 4,
            out_specs=(vmem,) * 3,
            scratch_shapes=[
                pltpu.VMEM(cpoints.shape, f32),
                pltpu.VMEM(weights.shape, bf16),
                pltpu.VMEM(coarse_gain.shape, f32),
                pltpu.VMEM(cotangent.shape, f32),
                dma((3 + layers,)),
                pltpu.VMEM((2, layers, width, pixels), bf16),
                pltpu.VMEM((2, layers) + state, f32),
                pltpu.VMEM((width, pixels), bf16),
                pltpu.VMEM((layers, channels, width), bf16),
                pltpu.VMEM((layers, channels, width), f32),
                pltpu.VMEM(state, f32),
                pltpu.VMEM(state, f32),
                pltpu.VMEM(state, f32),
                pltpu.VMEM(state, f32),
                pltpu.VMEM(state, f32),
                pltpu.VMEM((rounds, 8, 128), f32),
                pltpu.VMEM((rounds, 8, 128), f32),
                pltpu.VMEM((rounds,) + state, f32),
                pltpu.VMEM((rounds,) + state, f32),
                pltpu.VMEM((rounds + 1,) + state, f32),
                pltpu.VMEM((rounds,) + state, f32),
                pltpu.VMEM(half, f32),
                pltpu.VMEM(half, f32),
                pltpu.VMEM(half, f32),
                pltpu.VMEM(half, f32),
                dma((rounds,)),
                dma((rounds,)),
                dma((rounds,)),
                dma((rounds,)),
                dma((rounds,)),
                dma((rounds,)),
                dma((2,)),
                dma((2,)),
                dma((layers,)),
                dma((layers,)),
                dma((layers,)),
                dma((layers,)),
                dma((layers,)),
                dma((layers,)),
            ],
            compiler_params=pltpu.CompilerParams(
                collective_id=0, has_side_effects=True, vmem_limit_bytes=40 * 1024 * 1024
            ),
        )(*[
            pltpu.with_memory_space_constraint(x, pltpu.HBM)
            for x in (cpoints, weights, coarse_gain, cotangent)
        ])
        return pl.pallas_call(
            deliver,
            out_shape=results,
            in_specs=[vmem] * 3,
            out_specs=(hbm,) * 3,
            scratch_shapes=[dma((2 + layers,))],
            compiler_params=pltpu.CompilerParams(vmem_limit_bytes=8 * 1024 * 1024),
        )(*found)

    states = P("depth", "dp", None, None)
    blocks = P("depth", None, None)
    return jax.shard_map(
        step,
        mesh=mesh,
        in_specs=(states, blocks, P("depth", None), states),
        out_specs=(states, states, blocks),
        check_vma=False,
    )
```

```python
import functools

import jax
import jax.numpy as jnp
from jax import lax
from jax.experimental import pallas as pl
from jax.experimental.pallas import tpu as pltpu
from jax.sharding import PartitionSpec as P

MESH = pl.DeviceIdType.MESH
WID = 16
TAP_OFFSETS = [(-1, -1), (-1, 0), (-1, 1), (0, -1), (0, 0), (0, 1), (1, -1), (1, 0), (1, 1)]


def kernel(
    depth,
    dp,
    cp_hbm,
    w_hbm,
    gain_hbm,
    cot_hbm,
    corr_ref,
    gcp_ref,
    gw_ref,
    cp_ref,
    w_ref,
    gain_ref,
    cot_ref,
    in_sem,
    patches,
    slopes,
    back_patches,
    turned,
    start_grads,
    relaxed_buf,
    start_buf,
    back_buf,
    bar_buf,
    passed_buf,
    gains,
    gains_in,
    adj_out,
    adj_in,
    fwd,
    fwd_in,
    sum_a,
    sum_b,
    part_a,
    part_b,
    gain_send,
    gain_recv,
    adj_send,
    adj_recv,
    fwd_send,
    fwd_recv,
    edge_send,
    edge_recv,
    a_send,
    a_recv,
    b_send,
    b_recv,
    c_send,
    c_recv,
):
    layers, channels, width = w_ref.shape
    pixels = cp_ref.shape[-1]
    fetches = [
        pltpu.make_async_copy(cp_hbm, cp_ref, in_sem.at[0]),
        pltpu.make_async_copy(gain_hbm, gain_ref, in_sem.at[1]),
        pltpu.make_async_copy(cot_hbm, cot_ref, in_sem.at[2]),
    ]
    for layer in range(layers):
        fetches.append(
            pltpu.make_async_copy(w_hbm.at[layer], w_ref.at[layer], in_sem.at[3 + layer])
        )
    for fetch in fetches:
        fetch.start()
    half = channels // 2
    step_size = 1.0 / (layers * depth)
    hops = []
    while 2 ** len(hops) < depth:
        hops.append(2 ** len(hops))
    rounds = len(hops)
    me = lax.axis_index("depth")
    lane = lax.axis_index("dp")
    side = lane % 2
    sibling = lane + 1 - 2 * side
    across = (lane + 2) % dp

    barrier = pltpu.get_barrier_semaphore()
    count = 2
    for mate in (sibling, across):
        pl.semaphore_signal(barrier, inc=1, device_id={"dp": mate}, device_id_type=MESH)
    for hop in hops:
        ahead, behind = me + hop < depth, me >= hop
        count = count + jnp.where(ahead, 1, 0) + jnp.where(behind, 1, 0)

        @pl.when(ahead)
        def _():
            pl.semaphore_signal(barrier, inc=1, device_id={"depth": me + hop}, device_id_type=MESH)

        @pl.when(behind)
        def _():
            pl.semaphore_signal(barrier, inc=1, device_id={"depth": me - hop}, device_id_type=MESH)

    pixel = lax.broadcasted_iota(jnp.int32, (8, pixels), 1)
    row, column = pixel // WID, pixel % WID
    masks = []
    for a, b in TAP_OFFSETS:
        ok = (row + a >= 0) & (row + a < pixels // WID) & (column + b >= 0) & (column + b < WID)
        masks.append(jnp.where(ok, 1.0, 0.0)[None])

    def unfold(values, ref):
        for t, (a, b) in enumerate(TAP_OFFSETS):
            off = a * WID + b
            moved = values
            if off:
                moved = pltpu.roll(values, (-off) % pixels, 1).reshape(channels // 8, 8, pixels)
                moved = (moved * masks[t]).reshape(channels, pixels)
            ref[t * channels : (t + 1) * channels, :] = moved.astype(jnp.bfloat16)

    def forward_layer(u, layer, which):
        squashed = jnp.tanh(u)
        slopes[which, layer] = 1.0 - squashed * squashed
        unfold(squashed, patches.at[which, layer])
        mixed = jnp.dot(
            w_ref[layer], patches[which, layer], preferred_element_type=jnp.float32
        )
        return u + step_size * mixed

    def backward_layer(g, layer, which):
        scaled = step_size * g
        rounded = scaled.astype(jnp.bfloat16)
        unfold(rounded.astype(jnp.float32), back_patches)
        grads = lax.dot_general(
            rounded,
            patches[which, layer],
            (((1,), (1,)), ((), ())),
            preferred_element_type=jnp.float32,
        )
        spread = jnp.dot(turned[layer], back_patches[...], preferred_element_type=jnp.float32)
        return g + slopes[which, layer] * spread, grads

    def along(src, dst, send, recv, target):
        return pltpu.make_async_remote_copy(
            src_ref=src,
            dst_ref=dst,
            send_sem=send,
            recv_sem=recv,
            device_id=target,
            device_id_type=MESH,
        )

    def gain_copy(r):
        return along(
            gains.at[r], gains_in.at[r], gain_send.at[r], gain_recv.at[r], {"depth": me + hops[r]}
        )

    def adj_copy(r):
        return along(
            adj_out.at[r], adj_in.at[r], adj_send.at[r], adj_recv.at[r], {"depth": me - hops[r]}
        )

    def fwd_copy(r):
        return along(
            fwd.at[r], fwd_in.at[r], fwd_send.at[r], fwd_recv.at[r], {"depth": me + hops[r]}
        )

    def relaxed_copy():
        return along(relaxed_buf, start_buf, edge_send.at[0], edge_recv.at[0], {"depth": me + 1})

    def back_copy():
        return along(back_buf, bar_buf, edge_send.at[1], edge_recv.at[1], {"depth": me - 1})

    eye = lax.broadcasted_iota(jnp.int32, (channels, channels), 0) == lax.broadcasted_iota(
        jnp.int32, (channels, channels), 1
    )

    def gain_column(r):
        line = jnp.broadcast_to(gains[r, 0:1, 0:channels], (channels, channels))
        return jnp.sum(jnp.where(eye, line, 0.0), axis=1, keepdims=True)

    def start_adj(r):
        @pl.when(me >= hops[r])
        def _():
            adj_out[r] = gain_column(r) * (cot_ref[0, 0] + passed_buf[...])
            adj_copy(r).start()

    def take_gain(r):
        @pl.when(me >= hops[r])
        def _():
            gain_copy(r).wait_recv()
            gains[r + 1] = gains[r] * gains_in[r]

        @pl.when(me < hops[r])
        def _():
            gains[r + 1] = gains[r]

    def start_gain(r):
        @pl.when(me + hops[r] < depth)
        def _():
            gain_copy(r).start()

    def take_adj(r):
        @pl.when(me + hops[r] < depth)
        def _():
            adj_copy(r).wait_recv()
            passed_buf[...] = passed_buf[...] + adj_in[r]

    def start_fwd(r):
        @pl.when(me + hops[r] < depth)
        def _():
            fwd_copy(r).start()

    def take_fwd(r):
        @pl.when(me >= hops[r])
        def _():
            fwd_copy(r).wait_recv()
            fwd[r + 1] = fwd[r] + gain_column(r) * fwd_in[r]

        @pl.when(me < hops[r])
        def _():
            fwd[r + 1] = fwd[r]

    gains[0] = jnp.zeros_like(gains[0])
    fetches[1].wait()
    gains[0, 0:1, 0:channels] = gain_ref[...]
    passed_buf[...] = jnp.zeros_like(passed_buf)
    fetches[0].wait()
    own = cp_ref[0, 0]
    fetches[3].wait()
    u = forward_layer(own, 0, 0)
    pl.semaphore_wait(barrier, count)
    fetches[2].wait()
    start_adj(0)
    if rounds > 1:
        start_gain(0)
    for layer in range(1, layers):
        fetches[3 + layer].wait()
        u = forward_layer(u, layer, 0)
    relaxed_buf[...] = u

    @pl.when(me + 1 < depth)
    def _():
        relaxed_copy().start()

    one = jnp.where(eye, 1.0, 0.0).astype(jnp.bfloat16)
    def turn(layer):
        pieces = []
        for t in reversed(range(len(TAP_OFFSETS))):
            block = w_ref[layer, :, t * channels : (t + 1) * channels]
            pieces.append(
                lax.dot_general(
                    one, block, (((1,), (1,)), ((), ())), preferred_element_type=jnp.float32
                ).astype(jnp.bfloat16)
            )
        turned[layer] = jnp.concatenate(pieces, axis=1)

    turn(0)
    for r in range(rounds - 1):
        take_gain(r)
        if r + 1 < rounds - 1:
            start_gain(r + 1)
        take_adj(r)
        start_adj(r + 1)
        if r == 0:
            for layer in range(1, layers):
                turn(layer)

    @pl.when(me > 0)
    def _():
        relaxed_back = along(
            relaxed_buf, start_buf, edge_send.at[0], edge_recv.at[0], {"depth": me - 1}
        )
        relaxed_back.wait_recv()

    @pl.when(me == 0)
    def _():
        start_buf[...] = own

    u = start_buf[...]
    for layer in range(layers):
        u = forward_layer(u, layer, 1)
    fwd[0] = u - jnp.where(me == 0, 0.0, 1.0) * gain_column(0) * start_buf[...]
    start_fwd(0)
    take_adj(rounds - 1)

    g = cot_ref[0, 0] + passed_buf[...]
    for position, layer in enumerate(reversed(range(layers))):
        g, grads = backward_layer(g, layer, 1)
        start_grads[layer] = grads
        if position == layers - 2:
            take_fwd(0)
            if rounds > 1:
                start_fwd(1)
    back_buf[...] = g

    @pl.when(me > 0)
    def _():
        back_copy().start()

    for r in range(1, rounds - 1):
        take_fwd(r)
        start_fwd(r + 1)

    @pl.when(me + 1 < depth)
    def _():
        back_copy().wait_recv()

    @pl.when(me + 1 == depth)
    def _():
        bar_buf[...] = jnp.zeros_like(bar_buf)

    g = bar_buf[...] - passed_buf[...]

    mine = pl.ds(pl.multiple_of(side * half, half), half)
    other = pl.ds(pl.multiple_of((1 - side) * half, half), half)

    def a_copy(layer):
        return along(
            start_grads.at[layer, other],
            part_a.at[layer],
            a_send.at[layer],
            a_recv.at[layer],
            {"dp": sibling},
        )

    def b_copy(layer):
        return along(
            sum_a.at[layer], part_b.at[layer], b_send.at[layer], b_recv.at[layer], {"dp": across}
        )

    def c_copy(layer):
        return along(
            sum_b.at[layer],
            gw_ref.at[layer, mine],
            c_send.at[layer],
            c_recv.at[layer],
            {"dp": sibling},
        )

    def middle(layer):
        a_copy(layer).wait_recv()
        sum_a[layer] = start_grads[layer, mine, :] + part_a[layer]
        b_copy(layer).start()

    def last(layer):
        b_copy(layer).wait_recv()
        sum_b[layer] = sum_a[layer] + part_b[layer]
        c_copy(layer).start()
        gw_ref[layer, mine, :] = sum_b[layer]

    for layer in reversed(range(layers)):
        g, grads = backward_layer(g, layer, 0)
        start_grads[layer] = start_grads[layer] + grads
        a_copy(layer).start()
        if layer + 1 < layers:
            middle(layer + 1)
    gcp_ref[0, 0] = g + jnp.where(me == 0, 1.0, 0.0) * back_buf[...]
    if rounds > 1:
        take_fwd(rounds - 1)
    corr_ref[0, 0] = fwd[rounds]
    middle(0)
    for layer in reversed(range(layers)):
        last(layer)
    for layer in reversed(range(layers)):
        c_copy(layer).wait_recv()
        a_copy(layer).wait_send()
        b_copy(layer).wait_send()
        c_copy(layer).wait_send()

    for r in range(rounds):
        if r + 1 < rounds:

            @pl.when(me + hops[r] < depth)
            def _():
                gain_copy(r).wait_send()

        @pl.when(me >= hops[r])
        def _():
            adj_copy(r).wait_send()

        @pl.when(me + hops[r] < depth)
        def _():
            fwd_copy(r).wait_send()

    @pl.when(me + 1 < depth)
    def _():
        relaxed_copy().wait_send()

    @pl.when(me > 0)
    def _():
        back_copy().wait_send()


def deliver(corr_in, gcp_in, gw_in, corr_out, gcp_out, gw_out, sem):
    moves = [
        pltpu.make_async_copy(corr_in, corr_out, sem.at[0]),
        pltpu.make_async_copy(gcp_in, gcp_out, sem.at[1]),
    ]
    for layer in range(gw_in.shape[0]):
        moves.append(
            pltpu.make_async_copy(gw_in.at[layer], gw_out.at[layer], sem.at[2 + layer])
        )
    for move in moves:
        move.start()
    for move in moves:
        move.wait()


def solution(mesh):
    depth, dp = mesh.shape["depth"], mesh.shape["dp"]
    rounds = max(1, (depth - 1).bit_length())

    def step(cpoints, weights, coarse_gain, cotangent):
        layers, channels, width = weights.shape
        pixels = cpoints.shape[-1]
        state = (channels, pixels)
        half = (layers, channels // 2, width)
        f32, bf16 = jnp.float32, jnp.bfloat16
        dma = pltpu.SemaphoreType.DMA
        vmem = pl.BlockSpec(memory_space=pltpu.VMEM)
        hbm = pl.BlockSpec(memory_space=pltpu.HBM)
        results = (
            jax.ShapeDtypeStruct(cpoints.shape, f32),
            jax.ShapeDtypeStruct(cpoints.shape, f32),
            jax.ShapeDtypeStruct(weights.shape, f32),
        )
        found = pl.pallas_call(
            functools.partial(kernel, depth, dp),
            out_shape=results,
            in_specs=[hbm] * 4,
            out_specs=(vmem,) * 3,
            scratch_shapes=[
                pltpu.VMEM(cpoints.shape, f32),
                pltpu.VMEM(weights.shape, bf16),
                pltpu.VMEM(coarse_gain.shape, f32),
                pltpu.VMEM(cotangent.shape, f32),
                dma((3 + layers,)),
                pltpu.VMEM((2, layers, width, pixels), bf16),
                pltpu.VMEM((2, layers) + state, f32),
                pltpu.VMEM((width, pixels), bf16),
                pltpu.VMEM((layers, channels, width), bf16),
                pltpu.VMEM((layers, channels, width), f32),
                pltpu.VMEM(state, f32),
                pltpu.VMEM(state, f32),
                pltpu.VMEM(state, f32),
                pltpu.VMEM(state, f32),
                pltpu.VMEM(state, f32),
                pltpu.VMEM((rounds, 8, 128), f32),
                pltpu.VMEM((rounds, 8, 128), f32),
                pltpu.VMEM((rounds,) + state, f32),
                pltpu.VMEM((rounds,) + state, f32),
                pltpu.VMEM((rounds + 1,) + state, f32),
                pltpu.VMEM((rounds,) + state, f32),
                pltpu.VMEM(half, f32),
                pltpu.VMEM(half, f32),
                pltpu.VMEM(half, f32),
                pltpu.VMEM(half, f32),
                dma((rounds,)),
                dma((rounds,)),
                dma((rounds,)),
                dma((rounds,)),
                dma((rounds,)),
                dma((rounds,)),
                dma((2,)),
                dma((2,)),
                dma((layers,)),
                dma((layers,)),
                dma((layers,)),
                dma((layers,)),
                dma((layers,)),
                dma((layers,)),
            ],
            compiler_params=pltpu.CompilerParams(
                collective_id=0, has_side_effects=True, vmem_limit_bytes=40 * 1024 * 1024
            ),
        )(*[
            pltpu.with_memory_space_constraint(x, pltpu.HBM)
            for x in (cpoints, weights, coarse_gain, cotangent)
        ])
        return pl.pallas_call(
            deliver,
            out_shape=results,
            in_specs=[vmem] * 3,
            out_specs=(hbm,) * 3,
            scratch_shapes=[dma((2 + layers,))],
            compiler_params=pltpu.CompilerParams(vmem_limit_bytes=8 * 1024 * 1024),
        )(*found)

    states = P("depth", "dp", None, None)
    blocks = P("depth", None, None)
    return jax.shard_map(
        step,
        mesh=mesh,
        in_specs=(states, blocks, P("depth", None), states),
        out_specs=(states, states, blocks),
        check_vma=False,
    )
```

```python
import functools

import jax
import jax.numpy as jnp
from jax import lax
from jax.experimental import pallas as pl
from jax.experimental.pallas import tpu as pltpu
from jax.sharding import PartitionSpec as P

MESH = pl.DeviceIdType.MESH
WID = 16


def kernel(
    depth,
    dp,
    cp_hbm,
    w_hbm,
    gain_hbm,
    cot_hbm,
    corr_ref,
    gcp_ref,
    gw_ref,
    cp_ref,
    w_ref,
    gain_ref,
    cot_ref,
    in_sem,
    patches,
    slopes,
    back_patches,
    back_rows,
    stacked,
    turned,
    start_grads,
    relaxed_buf,
    start_buf,
    back_buf,
    bar_buf,
    passed_buf,
    gains,
    gains_in,
    adj_out,
    adj_in,
    fwd,
    fwd_in,
    sum_a,
    sum_b,
    part_a,
    part_b,
    gain_send,
    gain_recv,
    adj_send,
    adj_recv,
    fwd_send,
    fwd_recv,
    edge_send,
    edge_recv,
    a_send,
    a_recv,
    b_send,
    b_recv,
    c_send,
    c_recv,
):
    layers, channels, width = w_ref.shape
    pixels = cp_ref.shape[-1]
    fetches = [
        pltpu.make_async_copy(cp_hbm, cp_ref, in_sem.at[0]),
        pltpu.make_async_copy(gain_hbm, gain_ref, in_sem.at[1]),
        pltpu.make_async_copy(cot_hbm, cot_ref, in_sem.at[2]),
    ]
    for layer in range(layers):
        fetches.append(
            pltpu.make_async_copy(w_hbm.at[layer], w_ref.at[layer], in_sem.at[3 + layer])
        )
    for fetch in fetches:
        fetch.start()
    half = channels // 2
    step_size = 1.0 / (layers * depth)
    hops = []
    while 2 ** len(hops) < depth:
        hops.append(2 ** len(hops))
    rounds = len(hops)
    me = lax.axis_index("depth")
    lane = lax.axis_index("dp")
    side = lane % 2
    sibling = lane + 1 - 2 * side
    across = (lane + 2) % dp

    barrier = pltpu.get_barrier_semaphore()
    count = 2
    for mate in (sibling, across):
        pl.semaphore_signal(barrier, inc=1, device_id={"dp": mate}, device_id_type=MESH)
    for hop in hops:
        ahead, behind = me + hop < depth, me >= hop
        count = count + jnp.where(ahead, 1, 0) + jnp.where(behind, 1, 0)

        @pl.when(ahead)
        def _():
            pl.semaphore_signal(barrier, inc=1, device_id={"depth": me + hop}, device_id_type=MESH)

        @pl.when(behind)
        def _():
            pl.semaphore_signal(barrier, inc=1, device_id={"depth": me - hop}, device_id_type=MESH)

    pixel = lax.broadcasted_iota(jnp.int32, (8, pixels), 1)
    row, column = pixel // WID, pixel % WID
    row_ok, column_ok = {}, {}
    for a in (-1, 1):
        row_ok[a] = jnp.where((row + a >= 0) & (row + a < pixels // WID), 1.0, 0.0)[None]
        column_ok[a] = jnp.where((column + a >= 0) & (column + a < WID), 1.0, 0.0)[None]
    tall = 3 * channels
    blocks = [slice(n * channels, (n + 1) * channels) for n in range(3)]

    def moved(values, distance, mask):
        shifted = pltpu.roll(values, (-distance) % pixels, 1).reshape(channels // 8, 8, pixels)
        return (shifted * mask).reshape(channels, pixels)

    def by_rows(values, a):
        return moved(values, a * WID, row_ok[a])

    def by_columns(values, b):
        return moved(values, b, column_ok[b])

    def forward_layer(u, layer, which):
        squashed = jnp.tanh(u)
        slopes[which, layer] = 1.0 - squashed * squashed
        kept = patches.at[which, layer]
        kept[blocks[0], :] = by_columns(squashed, -1).astype(jnp.bfloat16)
        kept[blocks[1], :] = squashed.astype(jnp.bfloat16)
        kept[blocks[2], :] = by_columns(squashed, 1).astype(jnp.bfloat16)
        mixed = jnp.dot(stacked[layer], kept[...], preferred_element_type=jnp.float32)
        mixed = mixed[blocks[1]] + by_rows(mixed[blocks[0]], -1) + by_rows(mixed[blocks[2]], 1)
        return u + step_size * mixed

    def backward_layer(g, layer, which):
        rounded = (step_size * g).astype(jnp.bfloat16)
        wide = rounded.astype(jnp.float32)
        back_patches[blocks[0], :] = by_columns(wide, 1).astype(jnp.bfloat16)
        back_patches[blocks[1], :] = rounded
        back_patches[blocks[2], :] = by_columns(wide, -1).astype(jnp.bfloat16)
        spread = jnp.dot(turned[layer], back_patches[...], preferred_element_type=jnp.float32)
        back_rows[blocks[0], :] = by_rows(wide, 1).astype(jnp.bfloat16)
        back_rows[blocks[1], :] = rounded
        back_rows[blocks[2], :] = by_rows(wide, -1).astype(jnp.bfloat16)
        grads = lax.dot_general(
            back_rows[...],
            patches[which, layer],
            (((1,), (1,)), ((), ())),
            preferred_element_type=jnp.float32,
        )
        grads = jnp.concatenate([grads[block] for block in blocks], axis=1)
        spread = spread[blocks[1]] + by_rows(spread[blocks[0]], 1) + by_rows(spread[blocks[2]], -1)
        return g + slopes[which, layer] * spread, grads

    def stack(layer):
        for n in range(3):
            stacked[layer, blocks[n], :] = w_ref[layer, :, n * tall : (n + 1) * tall]

    def along(src, dst, send, recv, target):
        return pltpu.make_async_remote_copy(
            src_ref=src,
            dst_ref=dst,
            send_sem=send,
            recv_sem=recv,
            device_id=target,
            device_id_type=MESH,
        )

    def gain_copy(r):
        return along(
            gains.at[r], gains_in.at[r], gain_send.at[r], gain_recv.at[r], {"depth": me + hops[r]}
        )

    def adj_copy(r):
        return along(
            adj_out.at[r], adj_in.at[r], adj_send.at[r], adj_recv.at[r], {"depth": me - hops[r]}
        )

    def fwd_copy(r):
        return along(
            fwd.at[r], fwd_in.at[r], fwd_send.at[r], fwd_recv.at[r], {"depth": me + hops[r]}
        )

    def relaxed_copy():
        return along(relaxed_buf, start_buf, edge_send.at[0], edge_recv.at[0], {"depth": me + 1})

    def back_copy():
        return along(back_buf, bar_buf, edge_send.at[1], edge_recv.at[1], {"depth": me - 1})

    eye = lax.broadcasted_iota(jnp.int32, (channels, channels), 0) == lax.broadcasted_iota(
        jnp.int32, (channels, channels), 1
    )

    def gain_column(r):
        line = jnp.broadcast_to(gains[r, 0:1, 0:channels], (channels, channels))
        return jnp.sum(jnp.where(eye, line, 0.0), axis=1, keepdims=True)

    def start_adj(r):
        @pl.when(me >= hops[r])
        def _():
            adj_out[r] = gain_column(r) * (cot_ref[0, 0] + passed_buf[...])
            adj_copy(r).start()

    def take_gain(r):
        @pl.when(me >= hops[r])
        def _():
            gain_copy(r).wait_recv()
            gains[r + 1] = gains[r] * gains_in[r]

        @pl.when(me < hops[r])
        def _():
            gains[r + 1] = gains[r]

    def start_gain(r):
        @pl.when(me + hops[r] < depth)
        def _():
            gain_copy(r).start()

    def take_adj(r):
        @pl.when(me + hops[r] < depth)
        def _():
            adj_copy(r).wait_recv()
            passed_buf[...] = passed_buf[...] + adj_in[r]

    def start_fwd(r):
        @pl.when(me + hops[r] < depth)
        def _():
            fwd_copy(r).start()

    def take_fwd(r):
        @pl.when(me >= hops[r])
        def _():
            fwd_copy(r).wait_recv()
            fwd[r + 1] = fwd[r] + gain_column(r) * fwd_in[r]

        @pl.when(me < hops[r])
        def _():
            fwd[r + 1] = fwd[r]

    gains[0] = jnp.zeros_like(gains[0])
    fetches[1].wait()
    gains[0, 0:1, 0:channels] = gain_ref[...]
    passed_buf[...] = jnp.zeros_like(passed_buf)
    fetches[0].wait()
    own = cp_ref[0, 0]
    fetches[3].wait()
    stack(0)
    u = forward_layer(own, 0, 0)
    pl.semaphore_wait(barrier, count)
    fetches[2].wait()
    start_adj(0)
    if rounds > 1:
        start_gain(0)
    for layer in range(1, layers):
        fetches[3 + layer].wait()
        stack(layer)
        u = forward_layer(u, layer, 0)
    relaxed_buf[...] = u

    @pl.when(me + 1 < depth)
    def _():
        relaxed_copy().start()

    one = lax.broadcasted_iota(jnp.int32, (tall, tall), 0) == lax.broadcasted_iota(
        jnp.int32, (tall, tall), 1
    )
    one = jnp.where(one, 1.0, 0.0).astype(jnp.bfloat16)

    def turn(layer):
        for n in range(3):
            flipped = lax.dot_general(
                one,
                stacked[layer, blocks[n], :],
                (((1,), (1,)), ((), ())),
                preferred_element_type=jnp.float32,
            )
            turned[layer, blocks[n], :] = jnp.concatenate(
                [flipped[block] for block in blocks], axis=1
            ).astype(jnp.bfloat16)

    turn(0)
    for r in range(rounds - 1):
        take_gain(r)
        if r + 1 < rounds - 1:
            start_gain(r + 1)
        take_adj(r)
        start_adj(r + 1)
        if r == 0:
            for layer in range(1, layers):
                turn(layer)

    @pl.when(me > 0)
    def _():
        relaxed_back = along(
            relaxed_buf, start_buf, edge_send.at[0], edge_recv.at[0], {"depth": me - 1}
        )
        relaxed_back.wait_recv()

    @pl.when(me == 0)
    def _():
        start_buf[...] = own

    u = start_buf[...]
    for layer in range(layers):
        u = forward_layer(u, layer, 1)
    fwd[0] = u - jnp.where(me == 0, 0.0, 1.0) * gain_column(0) * start_buf[...]
    start_fwd(0)
    take_adj(rounds - 1)

    g = cot_ref[0, 0] + passed_buf[...]
    for position, layer in enumerate(reversed(range(layers))):
        g, grads = backward_layer(g, layer, 1)
        start_grads[layer] = grads
        if position == layers - 2:
            take_fwd(0)
            if rounds > 1:
                start_fwd(1)
    back_buf[...] = g

    @pl.when(me > 0)
    def _():
        back_copy().start()

    for r in range(1, rounds - 1):
        take_fwd(r)
        start_fwd(r + 1)

    @pl.when(me + 1 < depth)
    def _():
        back_copy().wait_recv()

    @pl.when(me + 1 == depth)
    def _():
        bar_buf[...] = jnp.zeros_like(bar_buf)

    g = bar_buf[...] - passed_buf[...]

    mine = pl.ds(pl.multiple_of(side * half, half), half)
    other = pl.ds(pl.multiple_of((1 - side) * half, half), half)

    def a_copy(layer):
        return along(
            start_grads.at[layer, other],
            part_a.at[layer],
            a_send.at[layer],
            a_recv.at[layer],
            {"dp": sibling},
        )

    def b_copy(layer):
        return along(
            sum_a.at[layer], part_b.at[layer], b_send.at[layer], b_recv.at[layer], {"dp": across}
        )

    def c_copy(layer):
        return along(
            sum_b.at[layer],
            gw_ref.at[layer, mine],
            c_send.at[layer],
            c_recv.at[layer],
            {"dp": sibling},
        )

    def middle(layer):
        a_copy(layer).wait_recv()
        sum_a[layer] = start_grads[layer, mine, :] + part_a[layer]
        b_copy(layer).start()

    def last(layer):
        b_copy(layer).wait_recv()
        sum_b[layer] = sum_a[layer] + part_b[layer]
        c_copy(layer).start()
        gw_ref[layer, mine, :] = sum_b[layer]

    for layer in reversed(range(layers)):
        g, grads = backward_layer(g, layer, 0)
        start_grads[layer] = start_grads[layer] + grads
        a_copy(layer).start()
        if layer + 1 < layers:
            middle(layer + 1)
    gcp_ref[0, 0] = g + jnp.where(me == 0, 1.0, 0.0) * back_buf[...]
    if rounds > 1:
        take_fwd(rounds - 1)
    corr_ref[0, 0] = fwd[rounds]
    middle(0)
    for layer in reversed(range(layers)):
        last(layer)
    for layer in reversed(range(layers)):
        c_copy(layer).wait_recv()
        a_copy(layer).wait_send()
        b_copy(layer).wait_send()
        c_copy(layer).wait_send()

    for r in range(rounds):
        if r + 1 < rounds:

            @pl.when(me + hops[r] < depth)
            def _():
                gain_copy(r).wait_send()

        @pl.when(me >= hops[r])
        def _():
            adj_copy(r).wait_send()

        @pl.when(me + hops[r] < depth)
        def _():
            fwd_copy(r).wait_send()

    @pl.when(me + 1 < depth)
    def _():
        relaxed_copy().wait_send()

    @pl.when(me > 0)
    def _():
        back_copy().wait_send()


def deliver(corr_in, gcp_in, gw_in, corr_out, gcp_out, gw_out, sem):
    moves = [
        pltpu.make_async_copy(corr_in, corr_out, sem.at[0]),
        pltpu.make_async_copy(gcp_in, gcp_out, sem.at[1]),
    ]
    for layer in range(gw_in.shape[0]):
        moves.append(
            pltpu.make_async_copy(gw_in.at[layer], gw_out.at[layer], sem.at[2 + layer])
        )
    for move in moves:
        move.start()
    for move in moves:
        move.wait()


def solution(mesh):
    depth, dp = mesh.shape["depth"], mesh.shape["dp"]
    rounds = max(1, (depth - 1).bit_length())

    def step(cpoints, weights, coarse_gain, cotangent):
        layers, channels, width = weights.shape
        pixels = cpoints.shape[-1]
        state = (channels, pixels)
        half = (layers, channels // 2, width)
        f32, bf16 = jnp.float32, jnp.bfloat16
        dma = pltpu.SemaphoreType.DMA
        vmem = pl.BlockSpec(memory_space=pltpu.VMEM)
        hbm = pl.BlockSpec(memory_space=pltpu.HBM)
        results = (
            jax.ShapeDtypeStruct(cpoints.shape, f32),
            jax.ShapeDtypeStruct(cpoints.shape, f32),
            jax.ShapeDtypeStruct(weights.shape, f32),
        )
        found = pl.pallas_call(
            functools.partial(kernel, depth, dp),
            out_shape=results,
            in_specs=[hbm] * 4,
            out_specs=(vmem,) * 3,
            scratch_shapes=[
                pltpu.VMEM(cpoints.shape, f32),
                pltpu.VMEM(weights.shape, bf16),
                pltpu.VMEM(coarse_gain.shape, f32),
                pltpu.VMEM(cotangent.shape, f32),
                dma((3 + layers,)),
                pltpu.VMEM((2, layers, width // 3, pixels), bf16),
                pltpu.VMEM((2, layers) + state, f32),
                pltpu.VMEM((width // 3, pixels), bf16),
                pltpu.VMEM((width // 3, pixels), bf16),
                pltpu.VMEM((layers, 3 * channels, width // 3), bf16),
                pltpu.VMEM((layers, 3 * channels, width // 3), bf16),
                pltpu.VMEM((layers, channels, width), f32),
                pltpu.VMEM(state, f32),
                pltpu.VMEM(state, f32),
                pltpu.VMEM(state, f32),
                pltpu.VMEM(state, f32),
                pltpu.VMEM(state, f32),
                pltpu.VMEM((rounds, 8, 128), f32),
                pltpu.VMEM((rounds, 8, 128), f32),
                pltpu.VMEM((rounds,) + state, f32),
                pltpu.VMEM((rounds,) + state, f32),
                pltpu.VMEM((rounds + 1,) + state, f32),
                pltpu.VMEM((rounds,) + state, f32),
                pltpu.VMEM(half, f32),
                pltpu.VMEM(half, f32),
                pltpu.VMEM(half, f32),
                pltpu.VMEM(half, f32),
                dma((rounds,)),
                dma((rounds,)),
                dma((rounds,)),
                dma((rounds,)),
                dma((rounds,)),
                dma((rounds,)),
                dma((2,)),
                dma((2,)),
                dma((layers,)),
                dma((layers,)),
                dma((layers,)),
                dma((layers,)),
                dma((layers,)),
                dma((layers,)),
            ],
            compiler_params=pltpu.CompilerParams(
                collective_id=0, has_side_effects=True, vmem_limit_bytes=40 * 1024 * 1024
            ),
        )(*[
            pltpu.with_memory_space_constraint(x, pltpu.HBM)
            for x in (cpoints, weights, coarse_gain, cotangent)
        ])
        return pl.pallas_call(
            deliver,
            out_shape=results,
            in_specs=[vmem] * 3,
            out_specs=(hbm,) * 3,
            scratch_shapes=[dma((2 + layers,))],
            compiler_params=pltpu.CompilerParams(vmem_limit_bytes=8 * 1024 * 1024),
        )(*found)

    states = P("depth", "dp", None, None)
    blocks = P("depth", None, None)
    return jax.shard_map(
        step,
        mesh=mesh,
        in_specs=(states, blocks, P("depth", None), states),
        out_specs=(states, states, blocks),
        check_vma=False,
    )
```

```python
import functools

import jax
import jax.numpy as jnp
from jax import lax
from jax.experimental import pallas as pl
from jax.experimental.pallas import tpu as pltpu
from jax.sharding import PartitionSpec as P

MESH = pl.DeviceIdType.MESH
WID = 16


def kernel(
    depth,
    dp,
    cp_hbm,
    w_hbm,
    gain_hbm,
    cot_hbm,
    corr_ref,
    gcp_ref,
    gw_ref,
    cp_ref,
    w_ref,
    gain_ref,
    cot_ref,
    in_sem,
    patches,
    slopes,
    both_patches,
    both_rows,
    stacked,
    turned,
    start_grads,
    own_grads,
    mate_cp,
    mate_passed,
    mate_bar,
    part_d,
    mate_send,
    mate_recv,
    d_send,
    d_recv,
    relaxed_buf,
    start_buf,
    back_buf,
    bar_buf,
    passed_buf,
    gains,
    gains_in,
    adj_out,
    adj_in,
    fwd,
    fwd_in,
    sum_a,
    sum_b,
    part_a,
    part_b,
    gain_send,
    gain_recv,
    adj_send,
    adj_recv,
    fwd_send,
    fwd_recv,
    edge_send,
    edge_recv,
    a_send,
    a_recv,
    b_send,
    b_recv,
    c_send,
    c_recv,
):
    layers, channels, width = w_ref.shape
    pixels = cp_ref.shape[-1]
    fetches = [
        pltpu.make_async_copy(cp_hbm, cp_ref, in_sem.at[0]),
        pltpu.make_async_copy(gain_hbm, gain_ref, in_sem.at[1]),
        pltpu.make_async_copy(cot_hbm, cot_ref, in_sem.at[2]),
    ]
    for layer in range(layers):
        fetches.append(
            pltpu.make_async_copy(w_hbm.at[layer], w_ref.at[layer], in_sem.at[3 + layer])
        )
    for fetch in fetches:
        fetch.start()
    half = channels // 2
    step_size = 1.0 / (layers * depth)
    hops = []
    while 2 ** len(hops) < depth:
        hops.append(2 ** len(hops))
    rounds = len(hops)
    me = lax.axis_index("depth")
    lane = lax.axis_index("dp")
    side = lane % 2
    sibling = lane + 1 - 2 * side
    across = (lane + 2) % dp

    barrier = pltpu.get_barrier_semaphore()
    count = 2
    for mate in (sibling, across):
        pl.semaphore_signal(barrier, inc=1, device_id={"dp": mate}, device_id_type=MESH)
    for hop in hops:
        ahead, behind = me + hop < depth, me >= hop
        count = count + jnp.where(ahead, 1, 0) + jnp.where(behind, 1, 0)

        @pl.when(ahead)
        def _():
            pl.semaphore_signal(barrier, inc=1, device_id={"depth": me + hop}, device_id_type=MESH)

        @pl.when(behind)
        def _():
            pl.semaphore_signal(barrier, inc=1, device_id={"depth": me - hop}, device_id_type=MESH)

    count = count + jnp.where(me + 1 < depth, 1, 0) + jnp.where(me > 0, 1, 0)

    @pl.when(me + 1 < depth)
    def _():
        pl.semaphore_signal(
            barrier, inc=1, device_id={"depth": me + 1, "dp": across}, device_id_type=MESH
        )

    @pl.when(me > 0)
    def _():
        pl.semaphore_signal(
            barrier, inc=1, device_id={"depth": me - 1, "dp": across}, device_id_type=MESH
        )

    pixel = lax.broadcasted_iota(jnp.int32, (8, pixels), 1)
    row, column = pixel // WID, pixel % WID
    row_ok, column_ok = {}, {}
    for a in (-1, 1):
        row_ok[a] = jnp.where((row + a >= 0) & (row + a < pixels // WID), 1.0, 0.0)[None]
        column_ok[a] = jnp.where((column + a >= 0) & (column + a < WID), 1.0, 0.0)[None]
    tall = 3 * channels
    blocks = [slice(n * channels, (n + 1) * channels) for n in range(3)]

    def moved(values, distance, mask):
        shifted = pltpu.roll(values, (-distance) % pixels, 1).reshape(channels // 8, 8, pixels)
        return (shifted * mask).reshape(channels, pixels)

    def by_rows(values, a):
        return moved(values, a * WID, row_ok[a])

    def by_columns(values, b):
        return moved(values, b, column_ok[b])

    def forward_layer(u, layer, which):
        squashed = jnp.tanh(u)
        slopes[which, layer] = 1.0 - squashed * squashed
        kept = patches.at[which, layer]
        kept[blocks[0], :] = by_columns(squashed, -1).astype(jnp.bfloat16)
        kept[blocks[1], :] = squashed.astype(jnp.bfloat16)
        kept[blocks[2], :] = by_columns(squashed, 1).astype(jnp.bfloat16)
        mixed = jnp.dot(stacked[layer], kept[...], preferred_element_type=jnp.float32)
        mixed = mixed[blocks[1]] + by_rows(mixed[blocks[0]], -1) + by_rows(mixed[blocks[2]], 1)
        return u + step_size * mixed

    def backward_layer(g, layer, which):
        back_patches, back_rows = both_patches.at[which // 2], both_rows.at[which // 2]
        rounded = (step_size * g).astype(jnp.bfloat16)
        wide = rounded.astype(jnp.float32)
        back_patches[blocks[0], :] = by_columns(wide, 1).astype(jnp.bfloat16)
        back_patches[blocks[1], :] = rounded
        back_patches[blocks[2], :] = by_columns(wide, -1).astype(jnp.bfloat16)
        spread = jnp.dot(turned[layer], back_patches[...], preferred_element_type=jnp.float32)
        back_rows[blocks[0], :] = by_rows(wide, 1).astype(jnp.bfloat16)
        back_rows[blocks[1], :] = rounded
        back_rows[blocks[2], :] = by_rows(wide, -1).astype(jnp.bfloat16)
        grads = lax.dot_general(
            back_rows[...],
            patches[which, layer],
            (((1,), (1,)), ((), ())),
            preferred_element_type=jnp.float32,
        )
        grads = jnp.concatenate([grads[block] for block in blocks], axis=1)
        spread = spread[blocks[1]] + by_rows(spread[blocks[0]], 1) + by_rows(spread[blocks[2]], -1)
        return g + slopes[which, layer] * spread, grads

    def stack(layer):
        for n in range(3):
            stacked[layer, blocks[n], :] = w_ref[layer, :, n * tall : (n + 1) * tall]

    def along(src, dst, send, recv, target):
        return pltpu.make_async_remote_copy(
            src_ref=src,
            dst_ref=dst,
            send_sem=send,
            recv_sem=recv,
            device_id=target,
            device_id_type=MESH,
        )

    def gain_copy(r):
        return along(
            gains.at[r], gains_in.at[r], gain_send.at[r], gain_recv.at[r], {"depth": me + hops[r]}
        )

    def adj_copy(r):
        return along(
            adj_out.at[r], adj_in.at[r], adj_send.at[r], adj_recv.at[r], {"depth": me - hops[r]}
        )

    def fwd_copy(r):
        return along(
            fwd.at[r], fwd_in.at[r], fwd_send.at[r], fwd_recv.at[r], {"depth": me + hops[r]}
        )

    def relaxed_copy():
        return along(relaxed_buf, start_buf, edge_send.at[0], edge_recv.at[0], {"depth": me + 1})

    def back_copy():
        return along(back_buf, bar_buf, edge_send.at[1], edge_recv.at[1], {"depth": me - 1})

    def mate_cp_copy():
        return along(
            cp_ref.at[0, 0], mate_cp, mate_send.at[0], mate_recv.at[0], {"dp": across}
        )

    def mate_passed_copy():
        return along(passed_buf, mate_passed, mate_send.at[1], mate_recv.at[1], {"dp": across})

    def mate_back_copy():
        return along(
            back_buf, mate_bar, mate_send.at[2], mate_recv.at[2], {"depth": me - 1, "dp": across}
        )

    eye = lax.broadcasted_iota(jnp.int32, (channels, channels), 0) == lax.broadcasted_iota(
        jnp.int32, (channels, channels), 1
    )

    def gain_column(r):
        line = jnp.broadcast_to(gains[r, 0:1, 0:channels], (channels, channels))
        return jnp.sum(jnp.where(eye, line, 0.0), axis=1, keepdims=True)

    def start_adj(r):
        @pl.when(me >= hops[r])
        def _():
            adj_out[r] = gain_column(r) * (cot_ref[0, 0] + passed_buf[...])
            adj_copy(r).start()

    def take_gain(r):
        @pl.when(me >= hops[r])
        def _():
            gain_copy(r).wait_recv()
            gains[r + 1] = gains[r] * gains_in[r]

        @pl.when(me < hops[r])
        def _():
            gains[r + 1] = gains[r]

    def start_gain(r):
        @pl.when(me + hops[r] < depth)
        def _():
            gain_copy(r).start()

    def take_adj(r):
        @pl.when(me + hops[r] < depth)
        def _():
            adj_copy(r).wait_recv()
            passed_buf[...] = passed_buf[...] + adj_in[r]

    def start_fwd(r):
        @pl.when(me + hops[r] < depth)
        def _():
            fwd_copy(r).start()

    def take_fwd(r):
        @pl.when(me >= hops[r])
        def _():
            fwd_copy(r).wait_recv()
            fwd[r + 1] = fwd[r] + gain_column(r) * fwd_in[r]

        @pl.when(me < hops[r])
        def _():
            fwd[r + 1] = fwd[r]

    gains[0] = jnp.zeros_like(gains[0])
    fetches[1].wait()
    gains[0, 0:1, 0:channels] = gain_ref[...]
    passed_buf[...] = jnp.zeros_like(passed_buf)
    fetches[0].wait()
    own = cp_ref[0, 0]
    fetches[3].wait()
    stack(0)
    u = forward_layer(own, 0, 0)
    pl.semaphore_wait(barrier, count)
    fetches[2].wait()
    start_adj(0)
    if rounds > 1:
        start_gain(0)
    mate_cp_copy().start()
    for layer in range(1, layers):
        fetches[3 + layer].wait()
        stack(layer)
        u = forward_layer(u, layer, 0)
    relaxed_buf[...] = u

    @pl.when(me + 1 < depth)
    def _():
        relaxed_copy().start()

    one = lax.broadcasted_iota(jnp.int32, (tall, tall), 0) == lax.broadcasted_iota(
        jnp.int32, (tall, tall), 1
    )
    one = jnp.where(one, 1.0, 0.0).astype(jnp.bfloat16)

    def turn(layer):
        for n in range(3):
            flipped = lax.dot_general(
                one,
                stacked[layer, blocks[n], :],
                (((1,), (1,)), ((), ())),
                preferred_element_type=jnp.float32,
            )
            turned[layer, blocks[n], :] = jnp.concatenate(
                [flipped[block] for block in blocks], axis=1
            ).astype(jnp.bfloat16)

    turn(0)
    for r in range(rounds - 1):
        take_gain(r)
        if r + 1 < rounds - 1:
            start_gain(r + 1)
        take_adj(r)
        start_adj(r + 1)
        if r == 0:
            for layer in range(1, layers):
                turn(layer)
            mate_cp_copy().wait_recv()
            v = mate_cp[...]
            for layer in range(layers):
                v = forward_layer(v, layer, 2)

    @pl.when(me > 0)
    def _():
        relaxed_back = along(
            relaxed_buf, start_buf, edge_send.at[0], edge_recv.at[0], {"depth": me - 1}
        )
        relaxed_back.wait_recv()

    @pl.when(me == 0)
    def _():
        start_buf[...] = own

    u = start_buf[...]
    for layer in range(layers):
        u = forward_layer(u, layer, 1)
    fwd[0] = u - jnp.where(me == 0, 0.0, 1.0) * gain_column(0) * start_buf[...]
    start_fwd(0)
    take_adj(rounds - 1)
    mate_passed_copy().start()

    mine = pl.ds(pl.multiple_of(side * half, half), half)
    other = pl.ds(pl.multiple_of((1 - side) * half, half), half)

    def a_copy(layer):
        return along(
            start_grads.at[layer, other],
            part_a.at[layer],
            a_send.at[layer],
            a_recv.at[layer],
            {"dp": sibling},
        )

    def b_copy(layer):
        return along(
            sum_a.at[layer], part_b.at[layer], b_send.at[layer], b_recv.at[layer], {"dp": across}
        )

    def c_copy(layer):
        return along(
            sum_b.at[layer],
            gw_ref.at[layer, mine],
            c_send.at[layer],
            c_recv.at[layer],
            {"dp": sibling},
        )

    def middle(layer):
        a_copy(layer).wait_recv()
        sum_a[layer] = start_grads[layer, mine, :] + part_a[layer]
        b_copy(layer).start()

    def d_copy(layer):
        return along(
            own_grads.at[layer, other],
            part_d.at[layer],
            d_send.at[layer],
            d_recv.at[layer],
            {"dp": sibling},
        )

    def last(layer):
        b_copy(layer).wait_recv()
        starts = sum_a[layer] + part_b[layer]
        d_copy(layer).wait_recv()
        sum_b[layer] = starts + (own_grads[layer, mine, :] + part_d[layer])
        c_copy(layer).start()
        gw_ref[layer, mine, :] = sum_b[layer]

    g = cot_ref[0, 0] + passed_buf[...]
    for position, layer in enumerate(reversed(range(layers))):
        g, grads = backward_layer(g, layer, 1)
        start_grads[layer] = grads
        a_copy(layer).start()
        if position == 2:
            middle(layer + 2)
        if position == layers - 2:
            take_fwd(0)
            if rounds > 1:
                start_fwd(1)
    back_buf[...] = g

    @pl.when(me > 0)
    def _():
        back_copy().start()
        mate_back_copy().start()

    for layer in reversed(range(layers - 1)):
        middle(layer)
    for r in range(1, rounds - 1):
        take_fwd(r)
        start_fwd(r + 1)

    @pl.when(me + 1 < depth)
    def _():
        back_copy().wait_recv()
        mate_back_copy().wait_recv()

    @pl.when(me + 1 == depth)
    def _():
        bar_buf[...] = jnp.zeros_like(bar_buf)
        mate_bar[...] = jnp.zeros_like(mate_bar)

    mate_passed_copy().wait_recv()
    g = bar_buf[...] - passed_buf[...]
    h = mate_bar[...] - mate_passed[...]

    for layer in reversed(range(layers)):
        g, grads = backward_layer(g, layer, 0)
        h, mate_grads = backward_layer(h, layer, 2)
        own_grads[layer] = grads + mate_grads
        d_copy(layer).start()
    gcp_ref[0, 0] = g + jnp.where(me == 0, 1.0, 0.0) * back_buf[...]
    if rounds > 1:
        take_fwd(rounds - 1)
    corr_ref[0, 0] = fwd[rounds]
    for layer in reversed(range(layers)):
        last(layer)
    for layer in reversed(range(layers)):
        c_copy(layer).wait_recv()
        a_copy(layer).wait_send()
        b_copy(layer).wait_send()
        c_copy(layer).wait_send()
        d_copy(layer).wait_send()
    mate_cp_copy().wait_send()
    mate_passed_copy().wait_send()

    for r in range(rounds):
        if r + 1 < rounds:

            @pl.when(me + hops[r] < depth)
            def _():
                gain_copy(r).wait_send()

        @pl.when(me >= hops[r])
        def _():
            adj_copy(r).wait_send()

        @pl.when(me + hops[r] < depth)
        def _():
            fwd_copy(r).wait_send()

    @pl.when(me + 1 < depth)
    def _():
        relaxed_copy().wait_send()

    @pl.when(me > 0)
    def _():
        back_copy().wait_send()
        mate_back_copy().wait_send()


def deliver(corr_in, gcp_in, gw_in, corr_out, gcp_out, gw_out, sem):
    moves = [
        pltpu.make_async_copy(corr_in, corr_out, sem.at[0]),
        pltpu.make_async_copy(gcp_in, gcp_out, sem.at[1]),
    ]
    for layer in range(gw_in.shape[0]):
        moves.append(
            pltpu.make_async_copy(gw_in.at[layer], gw_out.at[layer], sem.at[2 + layer])
        )
    for move in moves:
        move.start()
    for move in moves:
        move.wait()


def solution(mesh):
    depth, dp = mesh.shape["depth"], mesh.shape["dp"]
    rounds = max(1, (depth - 1).bit_length())

    def step(cpoints, weights, coarse_gain, cotangent):
        layers, channels, width = weights.shape
        pixels = cpoints.shape[-1]
        state = (channels, pixels)
        half = (layers, channels // 2, width)
        f32, bf16 = jnp.float32, jnp.bfloat16
        dma = pltpu.SemaphoreType.DMA
        vmem = pl.BlockSpec(memory_space=pltpu.VMEM)
        hbm = pl.BlockSpec(memory_space=pltpu.HBM)
        results = (
            jax.ShapeDtypeStruct(cpoints.shape, f32),
            jax.ShapeDtypeStruct(cpoints.shape, f32),
            jax.ShapeDtypeStruct(weights.shape, f32),
        )
        found = pl.pallas_call(
            functools.partial(kernel, depth, dp),
            out_shape=results,
            in_specs=[hbm] * 4,
            out_specs=(vmem,) * 3,
            scratch_shapes=[
                pltpu.VMEM(cpoints.shape, f32),
                pltpu.VMEM(weights.shape, bf16),
                pltpu.VMEM(coarse_gain.shape, f32),
                pltpu.VMEM(cotangent.shape, f32),
                dma((3 + layers,)),
                pltpu.VMEM((3, layers, width // 3, pixels), bf16),
                pltpu.VMEM((3, layers) + state, f32),
                pltpu.VMEM((2, width // 3, pixels), bf16),
                pltpu.VMEM((2, width // 3, pixels), bf16),
                pltpu.VMEM((layers, 3 * channels, width // 3), bf16),
                pltpu.VMEM((layers, 3 * channels, width // 3), bf16),
                pltpu.VMEM((layers, channels, width), f32),
                pltpu.VMEM((layers, channels, width), f32),
                pltpu.VMEM(state, f32),
                pltpu.VMEM(state, f32),
                pltpu.VMEM(state, f32),
                pltpu.VMEM(half, f32),
                dma((3,)),
                dma((3,)),
                dma((layers,)),
                dma((layers,)),
                pltpu.VMEM(state, f32),
                pltpu.VMEM(state, f32),
                pltpu.VMEM(state, f32),
                pltpu.VMEM(state, f32),
                pltpu.VMEM(state, f32),
                pltpu.VMEM((rounds, 8, 128), f32),
                pltpu.VMEM((rounds, 8, 128), f32),
                pltpu.VMEM((rounds,) + state, f32),
                pltpu.VMEM((rounds,) + state, f32),
                pltpu.VMEM((rounds + 1,) + state, f32),
                pltpu.VMEM((rounds,) + state, f32),
                pltpu.VMEM(half, f32),
                pltpu.VMEM(half, f32),
                pltpu.VMEM(half, f32),
                pltpu.VMEM(half, f32),
                dma((rounds,)),
                dma((rounds,)),
                dma((rounds,)),
                dma((rounds,)),
                dma((rounds,)),
                dma((rounds,)),
                dma((2,)),
                dma((2,)),
                dma((layers,)),
                dma((layers,)),
                dma((layers,)),
                dma((layers,)),
                dma((layers,)),
                dma((layers,)),
            ],
            compiler_params=pltpu.CompilerParams(
                collective_id=0, has_side_effects=True, vmem_limit_bytes=40 * 1024 * 1024
            ),
        )(*[
            pltpu.with_memory_space_constraint(x, pltpu.HBM)
            for x in (cpoints, weights, coarse_gain, cotangent)
        ])
        return pl.pallas_call(
            deliver,
            out_shape=results,
            in_specs=[vmem] * 3,
            out_specs=(hbm,) * 3,
            scratch_shapes=[dma((2 + layers,))],
            compiler_params=pltpu.CompilerParams(vmem_limit_bytes=8 * 1024 * 1024),
        )(*found)

    states = P("depth", "dp", None, None)
    blocks = P("depth", None, None)
    return jax.shard_map(
        step,
        mesh=mesh,
        in_specs=(states, blocks, P("depth", None), states),
        out_specs=(states, states, blocks),
        check_vma=False,
    )
```

```python
import functools

import jax
import jax.numpy as jnp
from jax import lax
from jax.experimental import pallas as pl
from jax.experimental.pallas import tpu as pltpu
from jax.sharding import PartitionSpec as P

MESH = pl.DeviceIdType.MESH
WID = 16


def kernel(
    depth,
    dp,
    cp_hbm,
    w_hbm,
    gain_hbm,
    cot_hbm,
    corr_ref,
    gcp_ref,
    gw_ref,
    cp_ref,
    w_ref,
    gain_ref,
    cot_ref,
    in_sem,
    patches,
    slopes,
    both_patches,
    both_rows,
    stacked,
    turned,
    start_grads,
    own_grads,
    mate_cp,
    mate_passed,
    mate_bar,
    part_d,
    mate_send,
    mate_recv,
    d_send,
    d_recv,
    relaxed_buf,
    start_buf,
    back_buf,
    bar_buf,
    passed_buf,
    gains,
    gains_in,
    adj_out,
    adj_in,
    fwd,
    fwd_in,
    sum_a,
    sum_b,
    part_a,
    part_b,
    gain_send,
    gain_recv,
    adj_send,
    adj_recv,
    fwd_send,
    fwd_recv,
    edge_send,
    edge_recv,
    a_send,
    a_recv,
    b_send,
    b_recv,
    c_send,
    c_recv,
):
    layers, channels, width = w_ref.shape
    pixels = cp_ref.shape[-1]
    fetches = [
        pltpu.make_async_copy(cp_hbm, cp_ref, in_sem.at[0]),
        pltpu.make_async_copy(gain_hbm, gain_ref, in_sem.at[1]),
        pltpu.make_async_copy(cot_hbm, cot_ref, in_sem.at[2]),
    ]
    for layer in range(layers):
        fetches.append(
            pltpu.make_async_copy(w_hbm.at[layer], w_ref.at[layer], in_sem.at[3 + layer])
        )
    for fetch in fetches:
        fetch.start()
    half = channels // 2
    step_size = 1.0 / (layers * depth)
    hops = []
    while 2 ** len(hops) < depth:
        hops.append(2 ** len(hops))
    rounds = len(hops)
    me = lax.axis_index("depth")
    lane = lax.axis_index("dp")
    side = lane % 2
    sibling = lane + 1 - 2 * side
    across = (lane + 2) % dp

    barrier = pltpu.get_barrier_semaphore()
    count = 2
    for mate in (sibling, across):
        pl.semaphore_signal(barrier, inc=1, device_id={"dp": mate}, device_id_type=MESH)
    for hop in hops:
        ahead, behind = me + hop < depth, me >= hop
        count = count + jnp.where(ahead, 1, 0) + jnp.where(behind, 1, 0)

        @pl.when(ahead)
        def _():
            pl.semaphore_signal(barrier, inc=1, device_id={"depth": me + hop}, device_id_type=MESH)

        @pl.when(behind)
        def _():
            pl.semaphore_signal(barrier, inc=1, device_id={"depth": me - hop}, device_id_type=MESH)

    count = count + jnp.where(me + 1 < depth, 1, 0) + jnp.where(me > 0, 1, 0)

    @pl.when(me + 1 < depth)
    def _():
        pl.semaphore_signal(
            barrier, inc=1, device_id={"depth": me + 1, "dp": across}, device_id_type=MESH
        )

    @pl.when(me > 0)
    def _():
        pl.semaphore_signal(
            barrier, inc=1, device_id={"depth": me - 1, "dp": across}, device_id_type=MESH
        )

    pixel = lax.broadcasted_iota(jnp.int32, (8, pixels), 1)
    row, column = pixel // WID, pixel % WID
    row_ok, column_ok = {}, {}
    for a in (-1, 1):
        row_ok[a] = jnp.where((row + a >= 0) & (row + a < pixels // WID), 1.0, 0.0)[None]
        column_ok[a] = jnp.where((column + a >= 0) & (column + a < WID), 1.0, 0.0)[None]
    tall = 3 * channels
    blocks = [slice(n * channels, (n + 1) * channels) for n in range(3)]

    def moved(values, distance, mask):
        shifted = pltpu.roll(values, (-distance) % pixels, 1).reshape(channels // 8, 8, pixels)
        return (shifted * mask).reshape(channels, pixels)

    def by_rows(values, a):
        return moved(values, a * WID, row_ok[a])

    def by_columns(values, b):
        return moved(values, b, column_ok[b])

    def forward_layer(u, layer, which):
        squashed = jnp.tanh(u)
        slopes[which, layer] = 1.0 - squashed * squashed
        kept = patches.at[which, layer]
        kept[blocks[0], :] = by_columns(squashed, -1).astype(jnp.bfloat16)
        kept[blocks[1], :] = squashed.astype(jnp.bfloat16)
        kept[blocks[2], :] = by_columns(squashed, 1).astype(jnp.bfloat16)
        mixed = jnp.dot(stacked[layer], kept[...], preferred_element_type=jnp.float32)
        mixed = mixed[blocks[1]] + by_rows(mixed[blocks[0]], -1) + by_rows(mixed[blocks[2]], 1)
        return u + step_size * mixed

    def backward_layer(g, layer, which):
        back_patches, back_rows = both_patches.at[which // 2], both_rows.at[which // 2]
        rounded = (step_size * g).astype(jnp.bfloat16)
        wide = rounded.astype(jnp.float32)
        back_patches[blocks[0], :] = by_columns(wide, 1).astype(jnp.bfloat16)
        back_patches[blocks[1], :] = rounded
        back_patches[blocks[2], :] = by_columns(wide, -1).astype(jnp.bfloat16)
        spread = jnp.dot(turned[layer], back_patches[...], preferred_element_type=jnp.float32)
        back_rows[blocks[0], :] = by_rows(wide, 1).astype(jnp.bfloat16)
        back_rows[blocks[1], :] = rounded
        back_rows[blocks[2], :] = by_rows(wide, -1).astype(jnp.bfloat16)
        grads = lax.dot_general(
            back_rows[...],
            patches[which, layer],
            (((1,), (1,)), ((), ())),
            preferred_element_type=jnp.float32,
        )
        grads = jnp.concatenate([grads[block] for block in blocks], axis=1)
        spread = spread[blocks[1]] + by_rows(spread[blocks[0]], 1) + by_rows(spread[blocks[2]], -1)
        return g + slopes[which, layer] * spread, grads

    def stack(layer):
        for n in range(3):
            stacked[layer, blocks[n], :] = w_ref[layer, :, n * tall : (n + 1) * tall]

    def along(src, dst, send, recv, target):
        return pltpu.make_async_remote_copy(
            src_ref=src,
            dst_ref=dst,
            send_sem=send,
            recv_sem=recv,
            device_id=target,
            device_id_type=MESH,
        )

    def gain_copy(r):
        return along(
            gains.at[r], gains_in.at[r], gain_send.at[r], gain_recv.at[r], {"depth": me + hops[r]}
        )

    parts = [slice(0, half), slice(half, channels)]

    def adj_copy(r, n):
        return along(
            adj_out.at[r, parts[n]],
            adj_in.at[r, parts[n]],
            adj_send.at[r, n],
            adj_recv.at[r, n],
            {"depth": me - hops[r]},
        )

    def fwd_copy(r):
        return along(
            fwd.at[r], fwd_in.at[r], fwd_send.at[r], fwd_recv.at[r], {"depth": me + hops[r]}
        )

    def relaxed_copy():
        return along(relaxed_buf, start_buf, edge_send.at[0], edge_recv.at[0], {"depth": me + 1})

    def back_copy():
        return along(back_buf, bar_buf, edge_send.at[1], edge_recv.at[1], {"depth": me - 1})

    def mate_cp_copy():
        return along(
            cp_ref.at[0, 0], mate_cp, mate_send.at[0], mate_recv.at[0], {"dp": across}
        )

    def mate_passed_copy():
        return along(passed_buf, mate_passed, mate_send.at[1], mate_recv.at[1], {"dp": across})

    def mate_back_copy():
        return along(
            back_buf, mate_bar, mate_send.at[2], mate_recv.at[2], {"depth": me - 1, "dp": across}
        )

    eye = lax.broadcasted_iota(jnp.int32, (channels, channels), 0) == lax.broadcasted_iota(
        jnp.int32, (channels, channels), 1
    )

    def gain_column(r):
        line = jnp.broadcast_to(gains[r, 0:1, 0:channels], (channels, channels))
        return jnp.sum(jnp.where(eye, line, 0.0), axis=1, keepdims=True)

    def start_adj(r, n):
        @pl.when(me >= hops[r])
        def _():
            here = parts[n]
            adj_out[r, here] = gain_column(r)[here] * (cot_ref[0, 0, here] + passed_buf[here])
            adj_copy(r, n).start()

    def take_gain(r):
        @pl.when(me >= hops[r])
        def _():
            gain_copy(r).wait_recv()
            gains[r + 1] = gains[r] * gains_in[r]

        @pl.when(me < hops[r])
        def _():
            gains[r + 1] = gains[r]

    def start_gain(r):
        @pl.when(me + hops[r] < depth)
        def _():
            gain_copy(r).start()

    def take_adj(r, n):
        @pl.when(me + hops[r] < depth)
        def _():
            adj_copy(r, n).wait_recv()
            here = parts[n]
            passed_buf[here] = passed_buf[here] + adj_in[r, here]

    def start_fwd(r):
        @pl.when(me + hops[r] < depth)
        def _():
            fwd_copy(r).start()

    def take_fwd(r):
        @pl.when(me >= hops[r])
        def _():
            fwd_copy(r).wait_recv()
            fwd[r + 1] = fwd[r] + gain_column(r) * fwd_in[r]

        @pl.when(me < hops[r])
        def _():
            fwd[r + 1] = fwd[r]

    gains[0] = jnp.zeros_like(gains[0])
    fetches[1].wait()
    gains[0, 0:1, 0:channels] = gain_ref[...]
    passed_buf[...] = jnp.zeros_like(passed_buf)
    fetches[0].wait()
    own = cp_ref[0, 0]
    fetches[3].wait()
    stack(0)
    u = forward_layer(own, 0, 0)
    pl.semaphore_wait(barrier, count)
    fetches[2].wait()
    for n in range(2):
        start_adj(0, n)
    if rounds > 1:
        start_gain(0)
    mate_cp_copy().start()
    for layer in range(1, layers):
        fetches[3 + layer].wait()
        stack(layer)
        u = forward_layer(u, layer, 0)
    relaxed_buf[...] = u

    @pl.when(me + 1 < depth)
    def _():
        relaxed_copy().start()

    one = lax.broadcasted_iota(jnp.int32, (tall, tall), 0) == lax.broadcasted_iota(
        jnp.int32, (tall, tall), 1
    )
    one = jnp.where(one, 1.0, 0.0).astype(jnp.bfloat16)

    def turn(layer):
        for n in range(3):
            flipped = lax.dot_general(
                one,
                stacked[layer, blocks[n], :],
                (((1,), (1,)), ((), ())),
                preferred_element_type=jnp.float32,
            )
            turned[layer, blocks[n], :] = jnp.concatenate(
                [flipped[block] for block in blocks], axis=1
            ).astype(jnp.bfloat16)

    turn(0)
    for r in range(rounds - 1):
        take_gain(r)
        if r + 1 < rounds - 1:
            start_gain(r + 1)
        for n in range(2):
            take_adj(r, n)
            start_adj(r + 1, n)
        if r == 0:
            for layer in range(1, layers):
                turn(layer)

    @pl.when(me > 0)
    def _():
        relaxed_back = along(
            relaxed_buf, start_buf, edge_send.at[0], edge_recv.at[0], {"depth": me - 1}
        )
        relaxed_back.wait_recv()

    @pl.when(me == 0)
    def _():
        start_buf[...] = own

    mate_cp_copy().wait_recv()
    u = start_buf[...]
    v = mate_cp[...]
    for layer in range(layers):
        u = forward_layer(u, layer, 1)
        v = forward_layer(v, layer, 2)
    fwd[0] = u - jnp.where(me == 0, 0.0, 1.0) * gain_column(0) * start_buf[...]
    start_fwd(0)
    for n in range(2):
        take_adj(rounds - 1, n)
    mate_passed_copy().start()

    mine = pl.ds(pl.multiple_of(side * half, half), half)
    other = pl.ds(pl.multiple_of((1 - side) * half, half), half)

    def a_copy(layer):
        return along(
            start_grads.at[layer, other],
            part_a.at[layer],
            a_send.at[layer],
            a_recv.at[layer],
            {"dp": sibling},
        )

    def b_copy(layer):
        return along(
            sum_a.at[layer], part_b.at[layer], b_send.at[layer], b_recv.at[layer], {"dp": across}
        )

    def c_copy(layer):
        return along(
            sum_b.at[layer],
            gw_ref.at[layer, mine],
            c_send.at[layer],
            c_recv.at[layer],
            {"dp": sibling},
        )

    def middle(layer):
        a_copy(layer).wait_recv()
        sum_a[layer] = start_grads[layer, mine, :] + part_a[layer]
        b_copy(layer).start()

    def d_copy(layer):
        return along(
            own_grads.at[layer, other],
            part_d.at[layer],
            d_send.at[layer],
            d_recv.at[layer],
            {"dp": sibling},
        )

    def last(layer):
        b_copy(layer).wait_recv()
        starts = sum_a[layer] + part_b[layer]
        d_copy(layer).wait_recv()
        sum_b[layer] = starts + (own_grads[layer, mine, :] + part_d[layer])
        c_copy(layer).start()
        gw_ref[layer, mine, :] = sum_b[layer]

    g = cot_ref[0, 0] + passed_buf[...]
    for position, layer in enumerate(reversed(range(layers))):
        g, grads = backward_layer(g, layer, 1)
        start_grads[layer] = grads
        a_copy(layer).start()
        if position == 2:
            middle(layer + 2)
        if position == layers - 2:
            take_fwd(0)
            if rounds > 1:
                start_fwd(1)
    back_buf[...] = g

    @pl.when(me > 0)
    def _():
        back_copy().start()
        mate_back_copy().start()

    for layer in reversed(range(layers - 1)):
        middle(layer)
    for r in range(1, rounds - 1):
        take_fwd(r)
        start_fwd(r + 1)

    @pl.when(me + 1 < depth)
    def _():
        back_copy().wait_recv()
        mate_back_copy().wait_recv()

    @pl.when(me + 1 == depth)
    def _():
        bar_buf[...] = jnp.zeros_like(bar_buf)
        mate_bar[...] = jnp.zeros_like(mate_bar)

    mate_passed_copy().wait_recv()
    g = bar_buf[...] - passed_buf[...]
    h = mate_bar[...] - mate_passed[...]

    for layer in reversed(range(layers)):
        g, grads = backward_layer(g, layer, 0)
        h, mate_grads = backward_layer(h, layer, 2)
        own_grads[layer] = grads + mate_grads
        d_copy(layer).start()
    gcp_ref[0, 0] = g + jnp.where(me == 0, 1.0, 0.0) * back_buf[...]
    for layer in reversed(range(layers)):
        last(layer)
    if rounds > 1:
        take_fwd(rounds - 1)
    corr_ref[0, 0] = fwd[rounds]
    for layer in reversed(range(layers)):
        c_copy(layer).wait_recv()
        a_copy(layer).wait_send()
        b_copy(layer).wait_send()
        c_copy(layer).wait_send()
        d_copy(layer).wait_send()
    mate_cp_copy().wait_send()
    mate_passed_copy().wait_send()

    for r in range(rounds):
        if r + 1 < rounds:

            @pl.when(me + hops[r] < depth)
            def _():
                gain_copy(r).wait_send()

        @pl.when(me >= hops[r])
        def _():
            for n in range(2):
                adj_copy(r, n).wait_send()

        @pl.when(me + hops[r] < depth)
        def _():
            fwd_copy(r).wait_send()

    @pl.when(me + 1 < depth)
    def _():
        relaxed_copy().wait_send()

    @pl.when(me > 0)
    def _():
        back_copy().wait_send()
        mate_back_copy().wait_send()


def deliver(corr_in, gcp_in, gw_in, corr_out, gcp_out, gw_out, sem):
    moves = [
        pltpu.make_async_copy(corr_in, corr_out, sem.at[0]),
        pltpu.make_async_copy(gcp_in, gcp_out, sem.at[1]),
    ]
    for layer in range(gw_in.shape[0]):
        moves.append(
            pltpu.make_async_copy(gw_in.at[layer], gw_out.at[layer], sem.at[2 + layer])
        )
    for move in moves:
        move.start()
    for move in moves:
        move.wait()


def solution(mesh):
    depth, dp = mesh.shape["depth"], mesh.shape["dp"]
    rounds = max(1, (depth - 1).bit_length())

    def step(cpoints, weights, coarse_gain, cotangent):
        layers, channels, width = weights.shape
        pixels = cpoints.shape[-1]
        state = (channels, pixels)
        half = (layers, channels // 2, width)
        f32, bf16 = jnp.float32, jnp.bfloat16
        dma = pltpu.SemaphoreType.DMA
        vmem = pl.BlockSpec(memory_space=pltpu.VMEM)
        hbm = pl.BlockSpec(memory_space=pltpu.HBM)
        results = (
            jax.ShapeDtypeStruct(cpoints.shape, f32),
            jax.ShapeDtypeStruct(cpoints.shape, f32),
            jax.ShapeDtypeStruct(weights.shape, f32),
        )
        found = pl.pallas_call(
            functools.partial(kernel, depth, dp),
            out_shape=results,
            in_specs=[hbm] * 4,
            out_specs=(vmem,) * 3,
            scratch_shapes=[
                pltpu.VMEM(cpoints.shape, f32),
                pltpu.VMEM(weights.shape, bf16),
                pltpu.VMEM(coarse_gain.shape, f32),
                pltpu.VMEM(cotangent.shape, f32),
                dma((3 + layers,)),
                pltpu.VMEM((3, layers, width // 3, pixels), bf16),
                pltpu.VMEM((3, layers) + state, f32),
                pltpu.VMEM((2, width // 3, pixels), bf16),
                pltpu.VMEM((2, width // 3, pixels), bf16),
                pltpu.VMEM((layers, 3 * channels, width // 3), bf16),
                pltpu.VMEM((layers, 3 * channels, width // 3), bf16),
                pltpu.VMEM((layers, channels, width), f32),
                pltpu.VMEM((layers, channels, width), f32),
                pltpu.VMEM(state, f32),
                pltpu.VMEM(state, f32),
                pltpu.VMEM(state, f32),
                pltpu.VMEM(half, f32),
                dma((3,)),
                dma((3,)),
                dma((layers,)),
                dma((layers,)),
                pltpu.VMEM(state, f32),
                pltpu.VMEM(state, f32),
                pltpu.VMEM(state, f32),
                pltpu.VMEM(state, f32),
                pltpu.VMEM(state, f32),
                pltpu.VMEM((rounds, 8, 128), f32),
                pltpu.VMEM((rounds, 8, 128), f32),
                pltpu.VMEM((rounds,) + state, f32),
                pltpu.VMEM((rounds,) + state, f32),
                pltpu.VMEM((rounds + 1,) + state, f32),
                pltpu.VMEM((rounds,) + state, f32),
                pltpu.VMEM(half, f32),
                pltpu.VMEM(half, f32),
                pltpu.VMEM(half, f32),
                pltpu.VMEM(half, f32),
                dma((rounds,)),
                dma((rounds,)),
                dma((rounds, 2)),
                dma((rounds, 2)),
                dma((rounds,)),
                dma((rounds,)),
                dma((2,)),
                dma((2,)),
                dma((layers,)),
                dma((layers,)),
                dma((layers,)),
                dma((layers,)),
                dma((layers,)),
                dma((layers,)),
            ],
            compiler_params=pltpu.CompilerParams(
                collective_id=0, has_side_effects=True, vmem_limit_bytes=40 * 1024 * 1024
            ),
        )(*[
            pltpu.with_memory_space_constraint(x, pltpu.HBM)
            for x in (cpoints, weights, coarse_gain, cotangent)
        ])
        return pl.pallas_call(
            deliver,
            out_shape=results,
            in_specs=[vmem] * 3,
            out_specs=(hbm,) * 3,
            scratch_shapes=[dma((2 + layers,))],
            compiler_params=pltpu.CompilerParams(vmem_limit_bytes=8 * 1024 * 1024),
        )(*found)

    states = P("depth", "dp", None, None)
    blocks = P("depth", None, None)
    return jax.shard_map(
        step,
        mesh=mesh,
        in_specs=(states, blocks, P("depth", None), states),
        out_specs=(states, states, blocks),
        check_vma=False,
    )
```

```python
import functools

import jax
import jax.numpy as jnp
from jax import lax
from jax.experimental import pallas as pl
from jax.experimental.pallas import tpu as pltpu
from jax.sharding import PartitionSpec as P

MESH = pl.DeviceIdType.MESH
WID = 16


def kernel(
    depth,
    dp,
    cp_hbm,
    w_hbm,
    gain_hbm,
    cot_hbm,
    corr_ref,
    gcp_ref,
    gw_ref,
    cp_ref,
    w_ref,
    gain_ref,
    cot_ref,
    in_sem,
    patches,
    slopes,
    both_patches,
    both_rows,
    stacked,
    turned,
    start_grads,
    own_grads,
    mate_cp,
    mate_cot,
    mate_start,
    mate_passed,
    mate_bar,
    part_d,
    mate_send,
    mate_recv,
    d_send,
    d_recv,
    relaxed_buf,
    start_buf,
    back_buf,
    bar_buf,
    passed_buf,
    gains,
    gains_in,
    adj_out,
    adj_in,
    fwd,
    fwd_in,
    sum_b,
    gain_send,
    gain_recv,
    adj_send,
    adj_recv,
    fwd_send,
    fwd_recv,
    edge_send,
    edge_recv,
    c_send,
    c_recv,
):
    layers, channels, width = w_ref.shape
    pixels = cp_ref.shape[-1]
    fetches = [
        pltpu.make_async_copy(cp_hbm, cp_ref, in_sem.at[0]),
        pltpu.make_async_copy(gain_hbm, gain_ref, in_sem.at[1]),
        pltpu.make_async_copy(cot_hbm, cot_ref, in_sem.at[2]),
    ]
    for layer in range(layers):
        fetches.append(
            pltpu.make_async_copy(w_hbm.at[layer], w_ref.at[layer], in_sem.at[3 + layer])
        )
    for fetch in fetches:
        fetch.start()
    half = channels // 2
    step_size = 1.0 / (layers * depth)
    hops = []
    while 2 ** len(hops) < depth:
        hops.append(2 ** len(hops))
    rounds = len(hops)
    me = lax.axis_index("depth")
    lane = lax.axis_index("dp")
    side = lane % 2
    sibling = lane + 1 - 2 * side
    across = (lane + 2) % dp

    barrier = pltpu.get_barrier_semaphore()
    count = 2
    for mate in (sibling, across):
        pl.semaphore_signal(barrier, inc=1, device_id={"dp": mate}, device_id_type=MESH)
    for hop in hops:
        ahead, behind = me + hop < depth, me >= hop
        count = count + jnp.where(ahead, 1, 0) + jnp.where(behind, 1, 0)

        @pl.when(ahead)
        def _():
            pl.semaphore_signal(barrier, inc=1, device_id={"depth": me + hop}, device_id_type=MESH)

        @pl.when(behind)
        def _():
            pl.semaphore_signal(barrier, inc=1, device_id={"depth": me - hop}, device_id_type=MESH)

    count = count + jnp.where(me + 1 < depth, 1, 0) + jnp.where(me > 0, 1, 0)

    @pl.when(me + 1 < depth)
    def _():
        pl.semaphore_signal(
            barrier, inc=1, device_id={"depth": me + 1, "dp": across}, device_id_type=MESH
        )

    @pl.when(me > 0)
    def _():
        pl.semaphore_signal(
            barrier, inc=1, device_id={"depth": me - 1, "dp": across}, device_id_type=MESH
        )

    pixel = lax.broadcasted_iota(jnp.int32, (8, pixels), 1)
    row, column = pixel // WID, pixel % WID
    row_ok, column_ok = {}, {}
    for a in (-1, 1):
        row_ok[a] = jnp.where((row + a >= 0) & (row + a < pixels // WID), 1.0, 0.0)[None]
        column_ok[a] = jnp.where((column + a >= 0) & (column + a < WID), 1.0, 0.0)[None]
    tall = 3 * channels
    blocks = [slice(n * channels, (n + 1) * channels) for n in range(3)]

    def moved(values, distance, mask):
        shifted = pltpu.roll(values, (-distance) % pixels, 1).reshape(channels // 8, 8, pixels)
        return (shifted * mask).reshape(channels, pixels)

    def by_rows(values, a):
        return moved(values, a * WID, row_ok[a])

    def by_columns(values, b):
        return moved(values, b, column_ok[b])

    def forward_layer(u, layer, which):
        squashed = jnp.tanh(u)
        slopes[which, layer] = 1.0 - squashed * squashed
        kept = patches.at[which, layer]
        kept[blocks[0], :] = by_columns(squashed, -1).astype(jnp.bfloat16)
        kept[blocks[1], :] = squashed.astype(jnp.bfloat16)
        kept[blocks[2], :] = by_columns(squashed, 1).astype(jnp.bfloat16)
        mixed = jnp.dot(stacked[layer], kept[...], preferred_element_type=jnp.float32)
        mixed = mixed[blocks[1]] + by_rows(mixed[blocks[0]], -1) + by_rows(mixed[blocks[2]], 1)
        return u + step_size * mixed

    def backward_layer(g, layer, which):
        back_patches, back_rows = both_patches.at[which // 2], both_rows.at[which // 2]
        rounded = (step_size * g).astype(jnp.bfloat16)
        wide = rounded.astype(jnp.float32)
        back_patches[blocks[0], :] = by_columns(wide, 1).astype(jnp.bfloat16)
        back_patches[blocks[1], :] = rounded
        back_patches[blocks[2], :] = by_columns(wide, -1).astype(jnp.bfloat16)
        spread = jnp.dot(turned[layer], back_patches[...], preferred_element_type=jnp.float32)
        back_rows[blocks[0], :] = by_rows(wide, 1).astype(jnp.bfloat16)
        back_rows[blocks[1], :] = rounded
        back_rows[blocks[2], :] = by_rows(wide, -1).astype(jnp.bfloat16)
        grads = lax.dot_general(
            back_rows[...],
            patches[which, layer],
            (((1,), (1,)), ((), ())),
            preferred_element_type=jnp.float32,
        )
        grads = jnp.concatenate([grads[block] for block in blocks], axis=1)
        spread = spread[blocks[1]] + by_rows(spread[blocks[0]], 1) + by_rows(spread[blocks[2]], -1)
        return g + slopes[which, layer] * spread, grads

    def stack(layer):
        for n in range(3):
            stacked[layer, blocks[n], :] = w_ref[layer, :, n * tall : (n + 1) * tall]

    def along(src, dst, send, recv, target):
        return pltpu.make_async_remote_copy(
            src_ref=src,
            dst_ref=dst,
            send_sem=send,
            recv_sem=recv,
            device_id=target,
            device_id_type=MESH,
        )

    def gain_copy(r):
        return along(
            gains.at[r], gains_in.at[r], gain_send.at[r], gain_recv.at[r], {"depth": me + hops[r]}
        )

    parts = [slice(0, half), slice(half, channels)]

    def adj_copy(r, n):
        return along(
            adj_out.at[r, parts[n]],
            adj_in.at[r, parts[n]],
            adj_send.at[r, n],
            adj_recv.at[r, n],
            {"depth": me - hops[r]},
        )

    def fwd_copy(r):
        return along(
            fwd.at[r], fwd_in.at[r], fwd_send.at[r], fwd_recv.at[r], {"depth": me + hops[r]}
        )

    def relaxed_copy():
        return along(relaxed_buf, start_buf, edge_send.at[0], edge_recv.at[0], {"depth": me + 1})

    def back_copy():
        return along(back_buf, bar_buf, edge_send.at[1], edge_recv.at[1], {"depth": me - 1})

    def mate_cp_copy():
        return along(
            cp_ref.at[0, 0], mate_cp, mate_send.at[0], mate_recv.at[0], {"dp": across}
        )

    def mate_cot_copy():
        return along(
            cot_ref.at[0, 0], mate_cot, mate_send.at[3], mate_recv.at[3], {"dp": across}
        )

    def mate_start_copy():
        return along(start_buf, mate_start, mate_send.at[4], mate_recv.at[4], {"dp": across})

    def mate_passed_copy():
        return along(passed_buf, mate_passed, mate_send.at[1], mate_recv.at[1], {"dp": across})

    def mate_back_copy():
        return along(
            back_buf, mate_bar, mate_send.at[2], mate_recv.at[2], {"depth": me - 1, "dp": across}
        )

    eye = lax.broadcasted_iota(jnp.int32, (channels, channels), 0) == lax.broadcasted_iota(
        jnp.int32, (channels, channels), 1
    )

    def gain_column(r):
        line = jnp.broadcast_to(gains[r, 0:1, 0:channels], (channels, channels))
        return jnp.sum(jnp.where(eye, line, 0.0), axis=1, keepdims=True)

    def start_adj(r, n):
        @pl.when(me >= hops[r])
        def _():
            here = parts[n]
            adj_out[r, here] = gain_column(r)[here] * (cot_ref[0, 0, here] + passed_buf[here])
            adj_copy(r, n).start()

    def take_gain(r):
        @pl.when(me >= hops[r])
        def _():
            gain_copy(r).wait_recv()
            gains[r + 1] = gains[r] * gains_in[r]

        @pl.when(me < hops[r])
        def _():
            gains[r + 1] = gains[r]

    def start_gain(r):
        @pl.when(me + hops[r] < depth)
        def _():
            gain_copy(r).start()

    def take_adj(r, n):
        @pl.when(me + hops[r] < depth)
        def _():
            adj_copy(r, n).wait_recv()
            here = parts[n]
            passed_buf[here] = passed_buf[here] + adj_in[r, here]

    def start_fwd(r):
        @pl.when(me + hops[r] < depth)
        def _():
            fwd_copy(r).start()

    def take_fwd(r):
        @pl.when(me >= hops[r])
        def _():
            fwd_copy(r).wait_recv()
            fwd[r + 1] = fwd[r] + gain_column(r) * fwd_in[r]

        @pl.when(me < hops[r])
        def _():
            fwd[r + 1] = fwd[r]

    gains[0] = jnp.zeros_like(gains[0])
    fetches[1].wait()
    gains[0, 0:1, 0:channels] = gain_ref[...]
    passed_buf[...] = jnp.zeros_like(passed_buf)
    fetches[0].wait()
    own = cp_ref[0, 0]
    fetches[3].wait()
    stack(0)
    u = forward_layer(own, 0, 0)
    pl.semaphore_wait(barrier, count)
    fetches[2].wait()
    for n in range(2):
        start_adj(0, n)
    if rounds > 1:
        start_gain(0)
    mate_cp_copy().start()
    mate_cot_copy().start()
    for layer in range(1, layers):
        fetches[3 + layer].wait()
        stack(layer)
        u = forward_layer(u, layer, 0)
    relaxed_buf[...] = u

    @pl.when(me + 1 < depth)
    def _():
        relaxed_copy().start()

    one = lax.broadcasted_iota(jnp.int32, (tall, tall), 0) == lax.broadcasted_iota(
        jnp.int32, (tall, tall), 1
    )
    one = jnp.where(one, 1.0, 0.0).astype(jnp.bfloat16)

    def turn(layer):
        for n in range(3):
            flipped = lax.dot_general(
                one,
                stacked[layer, blocks[n], :],
                (((1,), (1,)), ((), ())),
                preferred_element_type=jnp.float32,
            )
            turned[layer, blocks[n], :] = jnp.concatenate(
                [flipped[block] for block in blocks], axis=1
            ).astype(jnp.bfloat16)

    turn(0)
    for r in range(rounds - 1):
        take_gain(r)
        if r + 1 < rounds - 1:
            start_gain(r + 1)
        for n in range(2):
            take_adj(r, n)
            start_adj(r + 1, n)
        if r == 0:
            for layer in range(1, layers):
                turn(layer)

    @pl.when(me > 0)
    def _():
        relaxed_back = along(
            relaxed_buf, start_buf, edge_send.at[0], edge_recv.at[0], {"depth": me - 1}
        )
        relaxed_back.wait_recv()

    @pl.when(me == 0)
    def _():
        start_buf[...] = own

    mate_start_copy().start()
    mate_cp_copy().wait_recv()
    u = start_buf[...]
    v = mate_cp[...]
    for layer in range(layers):
        u = forward_layer(u, layer, 1)
        v = forward_layer(v, layer, 2)
    fwd[0] = u - jnp.where(me == 0, 0.0, 1.0) * gain_column(0) * start_buf[...]
    start_fwd(0)
    for n in range(2):
        take_adj(rounds - 1, n)
    mate_passed_copy().start()

    mine = pl.ds(pl.multiple_of(side * half, half), half)
    other = pl.ds(pl.multiple_of((1 - side) * half, half), half)

    def c_copy(layer):
        return along(
            sum_b.at[layer],
            gw_ref.at[layer, mine],
            c_send.at[layer],
            c_recv.at[layer],
            {"dp": sibling},
        )

    def d_copy(layer):
        return along(
            own_grads.at[layer, other],
            part_d.at[layer],
            d_send.at[layer],
            d_recv.at[layer],
            {"dp": sibling},
        )

    def last(layer):
        d_copy(layer).wait_recv()
        sum_b[layer] = own_grads[layer, mine, :] + part_d[layer]
        c_copy(layer).start()
        gw_ref[layer, mine, :] = sum_b[layer]

    g = cot_ref[0, 0] + passed_buf[...]
    for position, layer in enumerate(reversed(range(layers))):
        g, grads = backward_layer(g, layer, 1)
        start_grads[layer] = grads
        if position == layers - 2:
            take_fwd(0)
            if rounds > 1:
                start_fwd(1)
    back_buf[...] = g

    @pl.when(me > 0)
    def _():
        back_copy().start()
        mate_back_copy().start()

    for r in range(1, rounds - 1):
        take_fwd(r)
        start_fwd(r + 1)

    mate_start_copy().wait_recv()
    v = mate_start[...]
    for layer in range(layers):
        v = forward_layer(v, layer, 3)
    mate_cot_copy().wait_recv()
    mate_passed_copy().wait_recv()
    h = mate_cot[...] + mate_passed[...]
    for layer in reversed(range(layers)):
        h, mate_grads = backward_layer(h, layer, 3)
        start_grads[layer] = start_grads[layer] + mate_grads

    @pl.when(me + 1 < depth)
    def _():
        back_copy().wait_recv()
        mate_back_copy().wait_recv()

    @pl.when(me + 1 == depth)
    def _():
        bar_buf[...] = jnp.zeros_like(bar_buf)
        mate_bar[...] = jnp.zeros_like(mate_bar)

    g = bar_buf[...] - passed_buf[...]
    h = mate_bar[...] - mate_passed[...]

    for layer in reversed(range(layers)):
        g, grads = backward_layer(g, layer, 0)
        h, mate_grads = backward_layer(h, layer, 2)
        own_grads[layer] = start_grads[layer] + (grads + mate_grads)
        d_copy(layer).start()
    gcp_ref[0, 0] = g + jnp.where(me == 0, 1.0, 0.0) * back_buf[...]
    for layer in reversed(range(layers)):
        last(layer)
    if rounds > 1:
        take_fwd(rounds - 1)
    corr_ref[0, 0] = fwd[rounds]
    for layer in reversed(range(layers)):
        c_copy(layer).wait_recv()
        c_copy(layer).wait_send()
        d_copy(layer).wait_send()
    mate_cp_copy().wait_send()
    mate_cot_copy().wait_send()
    mate_start_copy().wait_send()
    mate_passed_copy().wait_send()

    for r in range(rounds):
        if r + 1 < rounds:

            @pl.when(me + hops[r] < depth)
            def _():
                gain_copy(r).wait_send()

        @pl.when(me >= hops[r])
        def _():
            for n in range(2):
                adj_copy(r, n).wait_send()

        @pl.when(me + hops[r] < depth)
        def _():
            fwd_copy(r).wait_send()

    @pl.when(me + 1 < depth)
    def _():
        relaxed_copy().wait_send()

    @pl.when(me > 0)
    def _():
        back_copy().wait_send()
        mate_back_copy().wait_send()


def deliver(corr_in, gcp_in, gw_in, corr_out, gcp_out, gw_out, sem):
    moves = [
        pltpu.make_async_copy(corr_in, corr_out, sem.at[0]),
        pltpu.make_async_copy(gcp_in, gcp_out, sem.at[1]),
    ]
    for layer in range(gw_in.shape[0]):
        moves.append(
            pltpu.make_async_copy(gw_in.at[layer], gw_out.at[layer], sem.at[2 + layer])
        )
    for move in moves:
        move.start()
    for move in moves:
        move.wait()


def solution(mesh):
    depth, dp = mesh.shape["depth"], mesh.shape["dp"]
    rounds = max(1, (depth - 1).bit_length())

    def step(cpoints, weights, coarse_gain, cotangent):
        layers, channels, width = weights.shape
        pixels = cpoints.shape[-1]
        state = (channels, pixels)
        half = (layers, channels // 2, width)
        f32, bf16 = jnp.float32, jnp.bfloat16
        dma = pltpu.SemaphoreType.DMA
        vmem = pl.BlockSpec(memory_space=pltpu.VMEM)
        hbm = pl.BlockSpec(memory_space=pltpu.HBM)
        results = (
            jax.ShapeDtypeStruct(cpoints.shape, f32),
            jax.ShapeDtypeStruct(cpoints.shape, f32),
            jax.ShapeDtypeStruct(weights.shape, f32),
        )
        found = pl.pallas_call(
            functools.partial(kernel, depth, dp),
            out_shape=results,
            in_specs=[hbm] * 4,
            out_specs=(vmem,) * 3,
            scratch_shapes=[
                pltpu.VMEM(cpoints.shape, f32),
                pltpu.VMEM(weights.shape, bf16),
                pltpu.VMEM(coarse_gain.shape, f32),
                pltpu.VMEM(cotangent.shape, f32),
                dma((3 + layers,)),
                pltpu.VMEM((4, layers, width // 3, pixels), bf16),
                pltpu.VMEM((4, layers) + state, f32),
                pltpu.VMEM((2, width // 3, pixels), bf16),
                pltpu.VMEM((2, width // 3, pixels), bf16),
                pltpu.VMEM((layers, 3 * channels, width // 3), bf16),
                pltpu.VMEM((layers, 3 * channels, width // 3), bf16),
                pltpu.VMEM((layers, channels, width), f32),
                pltpu.VMEM((layers, channels, width), f32),
                pltpu.VMEM(state, f32),
                pltpu.VMEM(state, f32),
                pltpu.VMEM(state, f32),
                pltpu.VMEM(state, f32),
                pltpu.VMEM(state, f32),
                pltpu.VMEM(half, f32),
                dma((5,)),
                dma((5,)),
                dma((layers,)),
                dma((layers,)),
                pltpu.VMEM(state, f32),
                pltpu.VMEM(state, f32),
                pltpu.VMEM(state, f32),
                pltpu.VMEM(state, f32),
                pltpu.VMEM(state, f32),
                pltpu.VMEM((rounds, 8, 128), f32),
                pltpu.VMEM((rounds, 8, 128), f32),
                pltpu.VMEM((rounds,) + state, f32),
                pltpu.VMEM((rounds,) + state, f32),
                pltpu.VMEM((rounds + 1,) + state, f32),
                pltpu.VMEM((rounds,) + state, f32),
                pltpu.VMEM(half, f32),
                dma((rounds,)),
                dma((rounds,)),
                dma((rounds, 2)),
                dma((rounds, 2)),
                dma((rounds,)),
                dma((rounds,)),
                dma((2,)),
                dma((2,)),
                dma((layers,)),
                dma((layers,)),
            ],
            compiler_params=pltpu.CompilerParams(
                collective_id=0, has_side_effects=True, vmem_limit_bytes=40 * 1024 * 1024
            ),
        )(*[
            pltpu.with_memory_space_constraint(x, pltpu.HBM)
            for x in (cpoints, weights, coarse_gain, cotangent)
        ])
        return pl.pallas_call(
            deliver,
            out_shape=results,
            in_specs=[vmem] * 3,
            out_specs=(hbm,) * 3,
            scratch_shapes=[dma((2 + layers,))],
            compiler_params=pltpu.CompilerParams(vmem_limit_bytes=8 * 1024 * 1024),
        )(*found)

    states = P("depth", "dp", None, None)
    blocks = P("depth", None, None)
    return jax.shard_map(
        step,
        mesh=mesh,
        in_specs=(states, blocks, P("depth", None), states),
        out_specs=(states, states, blocks),
        check_vma=False,
    )
```

```python
import functools

import jax
import jax.numpy as jnp
from jax import lax
from jax.experimental import pallas as pl
from jax.experimental.pallas import tpu as pltpu
from jax.sharding import PartitionSpec as P

MESH = pl.DeviceIdType.MESH
WID = 16


def kernel(
    depth,
    dp,
    cp_hbm,
    w_hbm,
    gain_hbm,
    cot_hbm,
    corr_ref,
    gcp_ref,
    gw_ref,
    cp_ref,
    w_ref,
    gain_ref,
    cot_ref,
    in_sem,
    patches,
    slopes,
    both_patches,
    both_rows,
    stacked,
    turned,
    start_grads,
    own_grads,
    mate_cp,
    mate_cot,
    mate_start,
    mate_passed,
    mate_bar,
    part_d,
    mate_send,
    mate_recv,
    d_send,
    d_recv,
    relaxed_buf,
    start_buf,
    back_buf,
    bar_buf,
    passed_buf,
    gains,
    gains_in,
    adj_out,
    adj_in,
    fwd,
    fwd_in,
    gain_send,
    gain_recv,
    adj_send,
    adj_recv,
    fwd_send,
    fwd_recv,
    edge_send,
    edge_recv,
):
    layers, channels, width = w_ref.shape
    pixels = cp_ref.shape[-1]
    fetches = [
        pltpu.make_async_copy(cp_hbm, cp_ref, in_sem.at[0]),
        pltpu.make_async_copy(gain_hbm, gain_ref, in_sem.at[1]),
        pltpu.make_async_copy(cot_hbm, cot_ref, in_sem.at[2]),
    ]
    for layer in range(layers):
        fetches.append(
            pltpu.make_async_copy(w_hbm.at[layer], w_ref.at[layer], in_sem.at[3 + layer])
        )
    for fetch in fetches:
        fetch.start()
    half = channels // 2
    step_size = 1.0 / (layers * depth)
    hops = []
    while 2 ** len(hops) < depth:
        hops.append(2 ** len(hops))
    rounds = len(hops)
    me = lax.axis_index("depth")
    lane = lax.axis_index("dp")
    sibling = lane + 1 - 2 * (lane % 2)
    across = (lane + 2) % dp

    barrier = pltpu.get_barrier_semaphore()
    count = 2
    for mate in (sibling, across):
        pl.semaphore_signal(barrier, inc=1, device_id={"dp": mate}, device_id_type=MESH)
    for hop in hops:
        ahead, behind = me + hop < depth, me >= hop
        count = count + jnp.where(ahead, 1, 0) + jnp.where(behind, 1, 0)

        @pl.when(ahead)
        def _():
            pl.semaphore_signal(barrier, inc=1, device_id={"depth": me + hop}, device_id_type=MESH)

        @pl.when(behind)
        def _():
            pl.semaphore_signal(barrier, inc=1, device_id={"depth": me - hop}, device_id_type=MESH)

    count = count + jnp.where(me + 1 < depth, 1, 0) + jnp.where(me > 0, 1, 0)

    @pl.when(me + 1 < depth)
    def _():
        pl.semaphore_signal(
            barrier, inc=1, device_id={"depth": me + 1, "dp": across}, device_id_type=MESH
        )

    @pl.when(me > 0)
    def _():
        pl.semaphore_signal(
            barrier, inc=1, device_id={"depth": me - 1, "dp": across}, device_id_type=MESH
        )

    pixel = lax.broadcasted_iota(jnp.int32, (8, pixels), 1)
    row, column = pixel // WID, pixel % WID
    row_ok, column_ok = {}, {}
    for a in (-1, 1):
        row_ok[a] = jnp.where((row + a >= 0) & (row + a < pixels // WID), 1.0, 0.0)[None]
        column_ok[a] = jnp.where((column + a >= 0) & (column + a < WID), 1.0, 0.0)[None]
    tall = 3 * channels
    blocks = [slice(n * channels, (n + 1) * channels) for n in range(3)]

    def moved(values, distance, mask):
        shifted = pltpu.roll(values, (-distance) % pixels, 1).reshape(channels // 8, 8, pixels)
        return (shifted * mask).reshape(channels, pixels)

    def by_rows(values, a):
        return moved(values, a * WID, row_ok[a])

    def by_columns(values, b):
        return moved(values, b, column_ok[b])

    def forward_layer(u, layer, which):
        squashed = jnp.tanh(u)
        slopes[which, layer] = 1.0 - squashed * squashed
        kept = patches.at[which, layer]
        kept[blocks[0], :] = by_columns(squashed, -1).astype(jnp.bfloat16)
        kept[blocks[1], :] = squashed.astype(jnp.bfloat16)
        kept[blocks[2], :] = by_columns(squashed, 1).astype(jnp.bfloat16)
        mixed = jnp.dot(stacked[layer], kept[...], preferred_element_type=jnp.float32)
        mixed = mixed[blocks[1]] + by_rows(mixed[blocks[0]], -1) + by_rows(mixed[blocks[2]], 1)
        return u + step_size * mixed

    def backward_layer(g, layer, which):
        back_patches, back_rows = both_patches.at[which // 2], both_rows.at[which // 2]
        rounded = (step_size * g).astype(jnp.bfloat16)
        wide = rounded.astype(jnp.float32)
        back_patches[blocks[0], :] = by_columns(wide, 1).astype(jnp.bfloat16)
        back_patches[blocks[1], :] = rounded
        back_patches[blocks[2], :] = by_columns(wide, -1).astype(jnp.bfloat16)
        spread = jnp.dot(turned[layer], back_patches[...], preferred_element_type=jnp.float32)
        back_rows[blocks[0], :] = by_rows(wide, 1).astype(jnp.bfloat16)
        back_rows[blocks[1], :] = rounded
        back_rows[blocks[2], :] = by_rows(wide, -1).astype(jnp.bfloat16)
        grads = lax.dot_general(
            back_rows[...],
            patches[which, layer],
            (((1,), (1,)), ((), ())),
            preferred_element_type=jnp.float32,
        )
        grads = jnp.concatenate([grads[block] for block in blocks], axis=1)
        spread = spread[blocks[1]] + by_rows(spread[blocks[0]], 1) + by_rows(spread[blocks[2]], -1)
        return g + slopes[which, layer] * spread, grads

    def stack(layer):
        for n in range(3):
            stacked[layer, blocks[n], :] = w_ref[layer, :, n * tall : (n + 1) * tall]

    def along(src, dst, send, recv, target):
        return pltpu.make_async_remote_copy(
            src_ref=src,
            dst_ref=dst,
            send_sem=send,
            recv_sem=recv,
            device_id=target,
            device_id_type=MESH,
        )

    def gain_copy(r):
        return along(
            gains.at[r], gains_in.at[r], gain_send.at[r], gain_recv.at[r], {"depth": me + hops[r]}
        )

    parts = [slice(0, half), slice(half, channels)]

    def adj_copy(r, n):
        return along(
            adj_out.at[r, parts[n]],
            adj_in.at[r, parts[n]],
            adj_send.at[r, n],
            adj_recv.at[r, n],
            {"depth": me - hops[r]},
        )

    def fwd_copy(r):
        return along(
            fwd.at[r], fwd_in.at[r], fwd_send.at[r], fwd_recv.at[r], {"depth": me + hops[r]}
        )

    def relaxed_copy():
        return along(relaxed_buf, start_buf, edge_send.at[0], edge_recv.at[0], {"depth": me + 1})

    def back_copy():
        return along(back_buf, bar_buf, edge_send.at[1], edge_recv.at[1], {"depth": me - 1})

    def mate_cp_copy():
        return along(
            cp_ref.at[0, 0], mate_cp, mate_send.at[0], mate_recv.at[0], {"dp": across}
        )

    def mate_cot_copy():
        return along(
            cot_ref.at[0, 0], mate_cot, mate_send.at[3], mate_recv.at[3], {"dp": across}
        )

    def mate_start_copy():
        return along(start_buf, mate_start, mate_send.at[4], mate_recv.at[4], {"dp": across})

    def mate_passed_copy():
        return along(passed_buf, mate_passed, mate_send.at[1], mate_recv.at[1], {"dp": across})

    def mate_back_copy():
        return along(
            back_buf, mate_bar, mate_send.at[2], mate_recv.at[2], {"depth": me - 1, "dp": across}
        )

    eye = lax.broadcasted_iota(jnp.int32, (channels, channels), 0) == lax.broadcasted_iota(
        jnp.int32, (channels, channels), 1
    )

    def gain_column(r):
        line = jnp.broadcast_to(gains[r, 0:1, 0:channels], (channels, channels))
        return jnp.sum(jnp.where(eye, line, 0.0), axis=1, keepdims=True)

    def start_adj(r, n):
        @pl.when(me >= hops[r])
        def _():
            here = parts[n]
            adj_out[r, here] = gain_column(r)[here] * (cot_ref[0, 0, here] + passed_buf[here])
            adj_copy(r, n).start()

    def take_gain(r):
        @pl.when(me >= hops[r])
        def _():
            gain_copy(r).wait_recv()
            gains[r + 1] = gains[r] * gains_in[r]

        @pl.when(me < hops[r])
        def _():
            gains[r + 1] = gains[r]

    def start_gain(r):
        @pl.when(me + hops[r] < depth)
        def _():
            gain_copy(r).start()

    def take_adj(r, n):
        @pl.when(me + hops[r] < depth)
        def _():
            adj_copy(r, n).wait_recv()
            here = parts[n]
            passed_buf[here] = passed_buf[here] + adj_in[r, here]

    def start_fwd(r):
        @pl.when(me + hops[r] < depth)
        def _():
            fwd_copy(r).start()

    def take_fwd(r):
        @pl.when(me >= hops[r])
        def _():
            fwd_copy(r).wait_recv()
            fwd[r + 1] = fwd[r] + gain_column(r) * fwd_in[r]

        @pl.when(me < hops[r])
        def _():
            fwd[r + 1] = fwd[r]

    gains[0] = jnp.zeros_like(gains[0])
    fetches[1].wait()
    gains[0, 0:1, 0:channels] = gain_ref[...]
    passed_buf[...] = jnp.zeros_like(passed_buf)
    fetches[0].wait()
    own = cp_ref[0, 0]
    fetches[3].wait()
    stack(0)
    u = forward_layer(own, 0, 0)
    pl.semaphore_wait(barrier, count)
    fetches[2].wait()
    for n in range(2):
        start_adj(0, n)
    if rounds > 1:
        start_gain(0)
    mate_cp_copy().start()
    mate_cot_copy().start()
    for layer in range(1, layers):
        fetches[3 + layer].wait()
        stack(layer)
        u = forward_layer(u, layer, 0)
    relaxed_buf[...] = u

    @pl.when(me + 1 < depth)
    def _():
        relaxed_copy().start()

    one = lax.broadcasted_iota(jnp.int32, (tall, tall), 0) == lax.broadcasted_iota(
        jnp.int32, (tall, tall), 1
    )
    one = jnp.where(one, 1.0, 0.0).astype(jnp.bfloat16)

    def turn(layer):
        for n in range(3):
            flipped = lax.dot_general(
                one,
                stacked[layer, blocks[n], :],
                (((1,), (1,)), ((), ())),
                preferred_element_type=jnp.float32,
            )
            turned[layer, blocks[n], :] = jnp.concatenate(
                [flipped[block] for block in blocks], axis=1
            ).astype(jnp.bfloat16)

    turn(0)
    for r in range(rounds - 1):
        take_gain(r)
        if r + 1 < rounds - 1:
            start_gain(r + 1)
        for n in range(2):
            take_adj(r, n)
            start_adj(r + 1, n)
        if r == 0:
            for layer in range(1, layers):
                turn(layer)

    @pl.when(me > 0)
    def _():
        relaxed_back = along(
            relaxed_buf, start_buf, edge_send.at[0], edge_recv.at[0], {"depth": me - 1}
        )
        relaxed_back.wait_recv()

    @pl.when(me == 0)
    def _():
        start_buf[...] = own

    mate_start_copy().start()
    mate_cp_copy().wait_recv()
    u = start_buf[...]
    v = mate_cp[...]
    for layer in range(layers):
        u = forward_layer(u, layer, 1)
        v = forward_layer(v, layer, 2)
    fwd[0] = u - jnp.where(me == 0, 0.0, 1.0) * gain_column(0) * start_buf[...]
    start_fwd(0)
    for n in range(2):
        take_adj(rounds - 1, n)
    mate_passed_copy().start()

    def d_copy(layer):
        return along(
            own_grads.at[layer],
            part_d.at[layer],
            d_send.at[layer],
            d_recv.at[layer],
            {"dp": sibling},
        )

    def last(layer):
        d_copy(layer).wait_recv()
        gw_ref[layer] = own_grads[layer] + part_d[layer]

    g = cot_ref[0, 0] + passed_buf[...]
    for position, layer in enumerate(reversed(range(layers))):
        g, grads = backward_layer(g, layer, 1)
        start_grads[layer] = grads
        if position == layers - 2:
            take_fwd(0)
            if rounds > 1:
                start_fwd(1)
    back_buf[...] = g

    @pl.when(me > 0)
    def _():
        back_copy().start()
        mate_back_copy().start()

    for r in range(1, rounds - 1):
        take_fwd(r)
        start_fwd(r + 1)

    mate_start_copy().wait_recv()
    v = mate_start[...]
    for layer in range(layers):
        v = forward_layer(v, layer, 3)
    mate_cot_copy().wait_recv()
    mate_passed_copy().wait_recv()
    h = mate_cot[...] + mate_passed[...]
    for layer in reversed(range(layers)):
        h, mate_grads = backward_layer(h, layer, 3)
        start_grads[layer] = start_grads[layer] + mate_grads

    @pl.when(me + 1 < depth)
    def _():
        back_copy().wait_recv()
        mate_back_copy().wait_recv()

    @pl.when(me + 1 == depth)
    def _():
        bar_buf[...] = jnp.zeros_like(bar_buf)
        mate_bar[...] = jnp.zeros_like(mate_bar)

    g = bar_buf[...] - passed_buf[...]
    h = mate_bar[...] - mate_passed[...]

    for layer in reversed(range(layers)):
        g, grads = backward_layer(g, layer, 0)
        h, mate_grads = backward_layer(h, layer, 2)
        own_grads[layer] = start_grads[layer] + (grads + mate_grads)
        d_copy(layer).start()
        if layer + 2 < layers:
            last(layer + 2)
    gcp_ref[0, 0] = g + jnp.where(me == 0, 1.0, 0.0) * back_buf[...]
    if rounds > 1:
        take_fwd(rounds - 1)
    corr_ref[0, 0] = fwd[rounds]
    for layer in reversed(range(min(2, layers))):
        last(layer)
    for layer in reversed(range(layers)):
        d_copy(layer).wait_send()
    mate_cp_copy().wait_send()
    mate_cot_copy().wait_send()
    mate_start_copy().wait_send()
    mate_passed_copy().wait_send()

    for r in range(rounds):
        if r + 1 < rounds:

            @pl.when(me + hops[r] < depth)
            def _():
                gain_copy(r).wait_send()

        @pl.when(me >= hops[r])
        def _():
            for n in range(2):
                adj_copy(r, n).wait_send()

        @pl.when(me + hops[r] < depth)
        def _():
            fwd_copy(r).wait_send()

    @pl.when(me + 1 < depth)
    def _():
        relaxed_copy().wait_send()

    @pl.when(me > 0)
    def _():
        back_copy().wait_send()
        mate_back_copy().wait_send()


def deliver(corr_in, gcp_in, gw_in, corr_out, gcp_out, gw_out, sem):
    moves = [
        pltpu.make_async_copy(corr_in, corr_out, sem.at[0]),
        pltpu.make_async_copy(gcp_in, gcp_out, sem.at[1]),
    ]
    for layer in range(gw_in.shape[0]):
        moves.append(
            pltpu.make_async_copy(gw_in.at[layer], gw_out.at[layer], sem.at[2 + layer])
        )
    for move in moves:
        move.start()
    for move in moves:
        move.wait()


def solution(mesh):
    depth, dp = mesh.shape["depth"], mesh.shape["dp"]
    rounds = max(1, (depth - 1).bit_length())

    def step(cpoints, weights, coarse_gain, cotangent):
        layers, channels, width = weights.shape
        pixels = cpoints.shape[-1]
        state = (channels, pixels)
        f32, bf16 = jnp.float32, jnp.bfloat16
        dma = pltpu.SemaphoreType.DMA
        vmem = pl.BlockSpec(memory_space=pltpu.VMEM)
        hbm = pl.BlockSpec(memory_space=pltpu.HBM)
        results = (
            jax.ShapeDtypeStruct(cpoints.shape, f32),
            jax.ShapeDtypeStruct(cpoints.shape, f32),
            jax.ShapeDtypeStruct(weights.shape, f32),
        )
        found = pl.pallas_call(
            functools.partial(kernel, depth, dp),
            out_shape=results,
            in_specs=[hbm] * 4,
            out_specs=(vmem,) * 3,
            scratch_shapes=[
                pltpu.VMEM(cpoints.shape, f32),
                pltpu.VMEM(weights.shape, bf16),
                pltpu.VMEM(coarse_gain.shape, f32),
                pltpu.VMEM(cotangent.shape, f32),
                dma((3 + layers,)),
                pltpu.VMEM((4, layers, width // 3, pixels), bf16),
                pltpu.VMEM((4, layers) + state, f32),
                pltpu.VMEM((2, width // 3, pixels), bf16),
                pltpu.VMEM((2, width // 3, pixels), bf16),
                pltpu.VMEM((layers, 3 * channels, width // 3), bf16),
                pltpu.VMEM((layers, 3 * channels, width // 3), bf16),
                pltpu.VMEM((layers, channels, width), f32),
                pltpu.VMEM((layers, channels, width), f32),
                pltpu.VMEM(state, f32),
                pltpu.VMEM(state, f32),
                pltpu.VMEM(state, f32),
                pltpu.VMEM(state, f32),
                pltpu.VMEM(state, f32),
                pltpu.VMEM((layers, channels, width), f32),
                dma((5,)),
                dma((5,)),
                dma((layers,)),
                dma((layers,)),
                pltpu.VMEM(state, f32),
                pltpu.VMEM(state, f32),
                pltpu.VMEM(state, f32),
                pltpu.VMEM(state, f32),
                pltpu.VMEM(state, f32),
                pltpu.VMEM((rounds, 8, 128), f32),
                pltpu.VMEM((rounds, 8, 128), f32),
                pltpu.VMEM((rounds,) + state, f32),
                pltpu.VMEM((rounds,) + state, f32),
                pltpu.VMEM((rounds + 1,) + state, f32),
                pltpu.VMEM((rounds,) + state, f32),
                dma((rounds,)),
                dma((rounds,)),
                dma((rounds, 2)),
                dma((rounds, 2)),
                dma((rounds,)),
                dma((rounds,)),
                dma((2,)),
                dma((2,)),
            ],
            compiler_params=pltpu.CompilerParams(
                collective_id=0, has_side_effects=True, vmem_limit_bytes=40 * 1024 * 1024
            ),
        )(*[
            pltpu.with_memory_space_constraint(x, pltpu.HBM)
            for x in (cpoints, weights, coarse_gain, cotangent)
        ])
        return pl.pallas_call(
            deliver,
            out_shape=results,
            in_specs=[vmem] * 3,
            out_specs=(hbm,) * 3,
            scratch_shapes=[dma((2 + layers,))],
            compiler_params=pltpu.CompilerParams(vmem_limit_bytes=8 * 1024 * 1024),
        )(*found)

    states = P("depth", "dp", None, None)
    blocks = P("depth", None, None)
    return jax.shard_map(
        step,
        mesh=mesh,
        in_specs=(states, blocks, P("depth", None), states),
        out_specs=(states, states, blocks),
        check_vma=False,
    )
```
